32 devices in a mesh: dev: 32 (over z, y, x, core).
Axes of the slice: x: 2, y: 2, z: 4, core: 2. Of those that a mesh axis runs over, the one named last changes fastest.
Arguments:
- vectors: bfloat16 [8, 524288], P(None, 'dev'), may hold values from -1.5 to 1.5
- points: float32 [3, 524288], P(None, 'dev'), may hold values from -4 to 4
- leaf_basis: bfloat16 [2048, 64, 256], P('dev'), may hold values from -0.375 to 0.375
- near_list: int32 [2048, 8], P('dev'), may hold values from -32 to 32, as said below
- far_list: int32 [1984, 4], P('dev'), may hold values from -32 to 32, as said below
- transfer: bfloat16 [2016, 64, 128], P('dev'), may hold values from -0.625 to 0.625
- skeleton: float32 [2016, 192], P('dev'), may hold values from -4 to 4
- transfer_top: bfloat16 [31, 64, 128], replicated, may hold values from -0.625 to 0.625
- skeleton_top: float32 [30, 192], replicated, may hold values from -4 to 4
Outputs:
- product: float32 [8, 524288], P(None, 'dev')
The draws below stay inside these ranges and needn't reach their ends.
Inputs may be any that keep to these rules, and one draw needn't show every extreme that they name: `near_list`: slot 0 of every row holds 0 (the leaf itself); every other slot holds 0 (empty) or a nonzero offset such that the leaf plus the offset is a leaf; the nonzero offsets of a row are distinct. `far_list`: rows follow the numbering of the transfer rows of levels 1 to log2(64) - 1. An entry is 0 (empty) or a nonzero offset of magnitude 2 or more and at most that level's clusters on one device, such that the cluster plus the offset is a cluster of the same level; the nonzero offsets of a row are distinct.
All inputs are finite; a program needn't handle non-finite values.
Results may differ from the reference program's by a relative error of at most 0.002.
Values may be sent and summed in bfloat16 or wider, within the bound.
A program may use at most 64 MiB of HBM per device.

```python
import jax
import jax.numpy as jnp
import numpy as np
from jax import lax

LEAF = 256
RANK = 64
RHS = 8
LEAF_DEV = 64
NEAR_SLOTS = 8
FAR_SLOTS = 4
LEAVES = 2048
POINTS = 524288
PARENTS = 2016
TOP_ROWS = 31
TOP_SKELETONS = 30
N_DEV = 32


def choose_offsets(key, candidates, allowed, wanted, width):
    column_count = candidates.shape[1]
    ranking = jax.random.randint(key, candidates.shape, 0, 1 << 20)
    column = jnp.arange(column_count, dtype=jnp.int32)[None, :]
    scores = jnp.where(allowed, ranking * column_count + column, -1 - column)
    taken_count = min(width, column_count)
    best_scores, best_index = lax.top_k(scores, taken_count)
    picked = jnp.take_along_axis(candidates, best_index, axis=1)
    keeping = (best_scores >= 0) & (jnp.arange(taken_count, dtype=jnp.int32)[None, :] < wanted[:, None])
    picked = jnp.where(keeping, picked, 0).astype(jnp.int32)
    if taken_count < width:
        picked = jnp.concatenate([picked, jnp.zeros((picked.shape[0], width - taken_count), jnp.int32)], axis=1)
    return picked


def draw_near_list(key, part):
    key = jax.random.fold_in(key, 11)
    leaf_total = LEAF_DEV * N_DEV
    reach_leaves = LEAF_DEV // 2
    column = np.arange(2 * reach_leaves)
    magnitude = column // 2 + 1
    offsets_row = np.where(column % 2 == 0, magnitude, -magnitude).astype(np.int32)
    leaf_ids = np.arange(leaf_total, dtype=np.int32)[:, None]
    candidates = np.broadcast_to(offsets_row[None, :], (leaf_total, 2 * reach_leaves)).astype(np.int32)
    allowed = (leaf_ids + candidates >= 0) & (leaf_ids + candidates < leaf_total)
    key_dense, key_count, key_pick = jax.random.split(key, 3)
    dense_device = jax.random.randint(key_dense, (N_DEV,), 0, 4) == 0
    ceiling = jnp.repeat(jnp.where(dense_device, NEAR_SLOTS - 1, 1), LEAF_DEV)
    wanted = jax.random.randint(key_count, (leaf_total,), 0, 1 << 20) % ceiling + 1
    extra_slots = choose_offsets(key_pick, jnp.asarray(candidates), jnp.asarray(allowed), wanted, NEAR_SLOTS - 1)
    return jnp.concatenate([jnp.zeros((leaf_total, 1), jnp.int32), extra_slots], axis=1)


def draw_far_list(key, part):
    key = jax.random.fold_in(key, 23)
    level_counts = []
    local_index = []
    for level_index in range(1, LEAF_DEV.bit_length() - 1):
        level_count = LEAF_DEV >> level_index
        level_counts.extend([level_count] * level_count)
        local_index.extend(range(level_count))
    level_counts = np.tile(np.asarray(level_counts, np.int64), N_DEV)
    local_index = np.tile(np.asarray(local_index, np.int64), N_DEV)
    device_ids = np.repeat(np.arange(N_DEV, dtype=np.int64), LEAF_DEV - 2)
    global_index = device_ids * level_counts + local_index
    column_count = LEAF_DEV - 2
    column = np.arange(column_count)
    magnitude = column // 2 + 2
    offsets_row = np.where(column % 2 == 0, magnitude, -magnitude)
    candidates = np.broadcast_to(offsets_row[None, :], (level_counts.shape[0], column_count))
    target = global_index[:, None] + candidates
    allowed = (magnitude[None, :] <= level_counts[:, None]) & (target >= 0) & (target < (level_counts * N_DEV)[:, None])
    key_count, key_pick = jax.random.split(key, 2)
    wanted = jax.random.randint(key_count, (level_counts.shape[0],), 1, FAR_SLOTS + 1)
    return choose_offsets(key_pick, jnp.asarray(candidates.astype(np.int32)), jnp.asarray(allowed), wanted, FAR_SLOTS)


def levels(key, dims, pieces, low, high):
    gain, own = 1.0, jax.random.fold_in(key, 6)
    for position, shards_of in pieces:
        steps = jnp.exp(jax.random.uniform(jax.random.fold_in(own, position), (shards_of,), jnp.float32, low / len(pieces), high / len(pieces)))
        gain = gain * jnp.repeat(steps, dims[position] // shards_of).reshape([-1 if axis == position else 1 for axis in range(len(dims))])
    return gain


def bell_draw(own_key, extent, scale, reach, shards=(), held_as=jnp.bfloat16):
    array = jax.random.normal(own_key, extent, jnp.float32) * scale
    if len(shards) > 0:
        array = levels(own_key, extent, shards, -0.22, 0.18) * array
    return jnp.clip(array, min=-reach, max=reach).astype(held_as)


def setup_inputs(seed: int = 0) -> dict:
    seeds = jax.random.split(jax.random.key(seed), 10)
    vectors = bell_draw(seeds[0], (RHS, POINTS), 0.25, 1.5, ((1, 32),))
    points = bell_draw(seeds[1], (3, POINTS), 1.0, 4.0, ((1, 32),), jnp.float32)
    leaf_basis = bell_draw(seeds[2], (LEAVES, RANK, LEAF), LEAF ** -0.5, 0.375, ((0, 32),))
    near_list = draw_near_list(jax.random.fold_in(seeds[9], 71), 0)
    far_list = draw_far_list(jax.random.fold_in(seeds[9], 71), 0)
    transfer = bell_draw(seeds[5], (PARENTS, RANK, 2 * RANK), (7 * RANK // 5) ** -0.5, 0.625, ((0, 32),))
    skeleton = bell_draw(seeds[6], (PARENTS, 3 * RANK), 1.0, 4.0, ((0, 32),), jnp.float32)
    transfer_top = bell_draw(seeds[7], (TOP_ROWS, RANK, 2 * RANK), (7 * RANK // 5) ** -0.5, 0.625)
    skeleton_top = bell_draw(seeds[8], (TOP_SKELETONS, 3 * RANK), 1.0, 4.0, (), jnp.float32)
    return {"vectors": vectors, "points": points, "leaf_basis": leaf_basis, "near_list": near_list, "far_list": far_list, "transfer": transfer, "skeleton": skeleton, "transfer_top": transfer_top, "skeleton_top": skeleton_top}


highest = lax.Precision.HIGHEST

def kernel_block(targets, sources):
    spacing = targets[..., 0, :, None] - sources[..., 0, None, :]
    squares = spacing * spacing
    for component in (1, 2):
        spacing = targets[..., component, :, None] - sources[..., component, None, :]
        squares = squares + spacing * spacing
    return jnp.exp(-jnp.sqrt(squares))

def join_children(children):
    pair_count = children.shape[0] // 2
    joined = children.reshape(pair_count, 2, children.shape[1], children.shape[2]).transpose(0, 2, 1, 3)
    return joined.reshape(pair_count, children.shape[1], 2 * children.shape[2])

def split_children(joined, rank_size):
    parent_count = joined.shape[0]
    halves = joined.reshape(parent_count, joined.shape[1], 2, rank_size).transpose(0, 2, 1, 3)
    return halves.reshape(2 * parent_count, joined.shape[1], rank_size)

def lift_level(children, matrices):
    return jnp.einsum('mkj,mrj->mkr', children.astype(jnp.float32), matrices.astype(jnp.float32), precision=highest)

def lower_level(parents, matrices):
    return jnp.einsum('mkr,mrj->mkj', parents, matrices.astype(jnp.float32), precision=highest)

def swap_pairs(values):
    pair_count = values.shape[0] // 2
    return values.reshape((pair_count, 2) + values.shape[1:])[:, ::-1].reshape(values.shape)

def couple_sibling(skeletons, coefficients):
    tile_block = kernel_block(skeletons, swap_pairs(skeletons))
    return jnp.einsum('mij,mkj->mki', tile_block, swap_pairs(coefficients), precision=highest)

def reference(vectors, points, leaf_basis, near_list, far_list, transfer, skeleton, transfer_top, skeleton_top):
    local_levels = LEAF_DEV.bit_length() - 1
    top_levels = N_DEV.bit_length() - 1
    leaf_total = LEAF_DEV * N_DEV
    leaf_vectors = vectors.reshape(RHS, leaf_total, LEAF)
    leaf_points = points.reshape(3, leaf_total, LEAF).transpose(1, 0, 2)

    def near_block(block_index):
        first_leaf = block_index * LEAF_DEV
        targets = first_leaf + jnp.arange(LEAF_DEV, dtype=jnp.int32)
        offsets = lax.dynamic_slice_in_dim(near_list, first_leaf, LEAF_DEV, 0)
        usable = (jnp.arange(NEAR_SLOTS, dtype=jnp.int32)[None, :] == 0) | (offsets != 0)
        partners = jnp.clip(targets[:, None] + offsets, 0, leaf_total - 1).astype(jnp.int32)
        own_points = lax.dynamic_slice_in_dim(leaf_points, first_leaf, LEAF_DEV, 0)[:, None]
        tile_block = kernel_block(own_points, leaf_points[partners])
        tile_block = jnp.where(usable[:, :, None, None], tile_block, 0.0).astype(jnp.bfloat16)
        tile_block = lax.optimization_barrier(tile_block).astype(jnp.float32)
        sources = leaf_vectors[:, partners].astype(jnp.float32)
        return jnp.einsum('bsij,kbsj->kbi', tile_block, sources, precision=highest)
    near_blocks = lax.map(near_block, jnp.arange(N_DEV, dtype=jnp.int32))
    near_part = near_blocks.transpose(1, 0, 2, 3).reshape(RHS, leaf_total, LEAF)
    coefficients = [jnp.einsum('kti,tri->tkr', leaf_vectors.astype(jnp.float32), leaf_basis.astype(jnp.float32), precision=highest)]
    local_transfer = transfer.reshape(N_DEV, LEAF_DEV - 1, RANK, 2 * RANK)
    local_skeleton = skeleton.reshape(N_DEV, LEAF_DEV - 1, 3, RANK)
    local_far = far_list.reshape(N_DEV, LEAF_DEV - 2, FAR_SLOTS)
    transfers = [None]
    skeletons = [None]
    far_lists = [None]
    for level_index in range(1, local_levels + 1):
        first_row = LEAF_DEV - (LEAF_DEV >> level_index - 1)
        level_count = LEAF_DEV >> level_index
        transfers.append(local_transfer[:, first_row:first_row + level_count].reshape(-1, RANK, 2 * RANK))
        skeletons.append(local_skeleton[:, first_row:first_row + level_count].reshape(-1, 3, RANK))
        if level_index < local_levels:
            far_lists.append(local_far[:, first_row:first_row + level_count].reshape(-1, FAR_SLOTS))
    for step_index in range(1, top_levels + 1):
        first_row = N_DEV - (N_DEV >> step_index - 1)
        level_count = N_DEV >> step_index
        transfers.append(transfer_top[first_row:first_row + level_count])
        if step_index < top_levels:
            skeletons.append(skeleton_top[first_row:first_row + level_count].reshape(level_count, 3, RANK))
    all_levels = local_levels + top_levels
    for level_index in range(1, all_levels):
        coefficients.append(lift_level(join_children(coefficients[-1]), transfers[level_index]))
    downward = jnp.zeros((1, RHS, RANK), jnp.float32)
    for level_index in range(all_levels - 1, -1, -1):
        downward = split_children(lower_level(downward, transfers[level_index + 1]), RANK)
        if level_index >= local_levels:
            downward = downward + couple_sibling(skeletons[level_index], coefficients[level_index])
        elif level_index >= 1:
            level_count = coefficients[level_index].shape[0]
            for slot_index in range(FAR_SLOTS):
                offsets = far_lists[level_index][:, slot_index]
                partners = jnp.clip(jnp.arange(level_count, dtype=jnp.int32) + offsets, 0, level_count - 1).astype(jnp.int32)
                tile_block = kernel_block(skeletons[level_index], skeletons[level_index][partners])
                tile_block = jnp.where((offsets != 0)[:, None, None], tile_block, 0.0)
                downward = downward + jnp.einsum('mij,mkj->mki', tile_block, coefficients[level_index][partners], precision=highest)
    far_part = jnp.einsum('tkr,tri->kti', downward, leaf_basis.astype(jnp.float32), precision=highest)
    return (near_part + far_part).reshape(RHS, leaf_total * LEAF)
```

```python
import functools
import math

import jax
import jax.numpy as jnp
from jax import lax
from jax.experimental import pallas as pl
from jax.experimental.pallas import tpu as pltpu
from jax.sharding import PartitionSpec as P

F32 = jnp.float32
BF16 = jnp.bfloat16
LOG2E = math.log2(math.e)
TINY = 1e-30
FEATURES = 48
GROUP = 4
VMEM_BYTES = 56 * 1024 * 1024


def neighbours(cells):
    count = lax.axis_size("dev")
    ends = count - 1
    from_left = lax.ppermute(cells, "dev", [(i, i + 1) for i in range(ends)])
    from_right = lax.ppermute(cells, "dev", [(i + 1, i) for i in range(ends)])
    return from_left, from_right


def loop(count, unroll, step):
    unroll = min(unroll, count)

    def several(index, carry):
        for part in range(unroll):
            step(index * unroll + part)
        return carry

    lax.fori_loop(0, count // unroll, several, 0)


def level_row(leaf_count, level):
    return leaf_count - (leaf_count >> (level - 1))


def three_pieces(values):
    first = values.astype(BF16).astype(F32)
    rest = values - first
    second = rest.astype(BF16).astype(F32)
    return first, second, rest - second


def distance_factors(cells):
    scaled = cells * LOG2E
    norms = jnp.sum(scaled * scaled, axis=0, keepdims=True)
    row = lax.broadcasted_iota(jnp.int32, scaled.shape, 0)
    source = jnp.where(row == 3, norms, jnp.where(row == 4, 1.0, scaled))
    target = jnp.where(row == 3, 1.0, jnp.where(row == 4, norms, -2.0 * scaled))
    s1, s2, s3 = three_pieces(source)
    t1, t2, t3 = three_pieces(target)
    sources = jnp.concatenate([s1, s1, s2, s2, s1, s3], axis=0).astype(BF16)
    targets = jnp.concatenate([t1, t2, t1, t2, t3, t1], axis=0).astype(BF16)
    return sources, targets


def decay(squares):
    kept = jnp.maximum(squares, TINY)
    return jnp.exp2(-(kept * lax.rsqrt(kept)))


def product_rows(left, right):
    return lax.dot_general(left, right, (((0,), (0,)), ((), ())), preferred_element_type=F32)


def product(left, right):
    return lax.dot_general(left, right, (((1,), (0,)), ((), ())), preferred_element_type=F32)


def product_across(left, right):
    return lax.dot_general(left, right, (((1,), (1,)), ((), ())), preferred_element_type=F32)


def two_pieces(values):
    first = values.astype(BF16).astype(F32)
    return jnp.concatenate([first, values - first], axis=0).astype(BF16)


def fold(values):
    half = values.shape[0] // 2
    return values[:half] + values[half:]


def skeleton_cells(row):
    rank = row.shape[1] // 3
    parts = [row[:, c * rank : (c + 1) * rank] for c in range(3)]
    return jnp.concatenate(parts + [jnp.zeros((5, rank), F32)], axis=0)


def up_kernel(vec_ref, basis_ref, transfer_ref, skeleton_ref, table_ref, pair_ref):
    leaf_dev, rank, leaf = basis_ref.shape
    local = leaf_dev.bit_length() - 1

    def leaf_pair(pair):
        halves = []
        for part in range(2):
            spot = pair * 2 + part
            own = vec_ref[:, pl.ds(pl.multiple_of(spot * leaf, leaf), leaf)]
            halves.append(product_across(own, basis_ref[spot]))
        pair_ref[pair] = jnp.concatenate(halves, axis=1)

    loop(leaf_dev // 2, 8, leaf_pair)
    joined = [pair_ref[pair] for pair in range(leaf_dev // 2)]
    for level in range(1, local + 1):
        first = level_row(leaf_dev, level)
        coefs = []
        for spot in range(leaf_dev >> level):
            coef = fold(product_across(two_pieces(joined[spot]), transfer_ref[first + spot]))
            cells = skeleton_cells(skeleton_ref[pl.ds(first + spot, 1), :])
            table_ref[first + spot] = jnp.concatenate([coef, cells], axis=1)
            coefs.append(coef)
        joined = [
            jnp.concatenate(coefs[2 * spot : 2 * spot + 2], axis=1)
            for spot in range(len(coefs) // 2)
        ]


def near_kernel(
    list_ref,
    points_ref,
    points_left_ref,
    points_right_ref,
    vec_ref,
    vec_left_ref,
    vec_right_ref,
    out_ref,
    source_ref,
    target_ref,
    wide_vec_ref,
    task_target_ref,
    task_source_ref,
):
    leaf_dev, slots = list_ref.shape
    leaf = points_ref.shape[1] // leaf_dev
    reach = leaf_dev // 2
    wide = leaf_dev + 2 * reach
    chunk = 4 * leaf

    def cells_of(ref, start):
        part = ref[:, pl.ds(start, chunk)]
        return jnp.concatenate([part, jnp.zeros((5, chunk), F32)], axis=0)

    def fill(points, vecs, base, own):
        def step(index):
            start = pl.multiple_of(index * chunk, chunk)
            spot = pl.multiple_of(base + start, chunk)
            sources, targets = distance_factors(cells_of(points, start))
            source_ref[:, pl.ds(spot, chunk)] = sources
            if own:
                target_ref[:, pl.ds(start, chunk)] = targets
                out_ref[:, pl.ds(start, chunk)] = jnp.zeros((out_ref.shape[0], chunk), F32)
            wide_vec_ref[:, pl.ds(spot, chunk)] = vecs[:, pl.ds(start, chunk)].astype(F32)

        loop(points.shape[1] // chunk, 2, step)

    fill(points_left_ref, vec_left_ref, 0, False)
    fill(points_ref, vec_ref, reach * leaf, True)
    fill(points_right_ref, vec_right_ref, (reach + leaf_dev) * leaf, False)
    empty = pl.ds(wide * leaf, leaf)
    source_ref[:, empty] = jnp.zeros((FEATURES, leaf), BF16)
    wide_vec_ref[:, empty] = jnp.zeros((wide_vec_ref.shape[0], leaf), F32)

    def enlist(target, count):
        for slot in range(slots):
            offset = list_ref[target, slot]
            task_target_ref[count] = target
            task_source_ref[count] = target + offset + reach
            if slot == 0:
                count = count + 1
            else:
                count = count + jnp.where(offset != 0, 1, 0)
        return count

    count = lax.fori_loop(0, leaf_dev, enlist, 0)
    for extra in range(GROUP):
        task_target_ref[count + extra] = 0
        task_source_ref[count + extra] = wide

    def several(index, carry):
        results = []
        for part in range(GROUP):
            target = pl.multiple_of(task_target_ref[index * GROUP + part] * leaf, leaf)
            source = pl.multiple_of(task_source_ref[index * GROUP + part] * leaf, leaf)
            squares = product_rows(
                source_ref[:, pl.ds(source, leaf)], target_ref[:, pl.ds(target, leaf)]
            )
            tile = decay(squares).astype(BF16)
            vec = wide_vec_ref[:, pl.ds(source, leaf)].astype(BF16)
            results.append((target, product(vec, tile)))
        for target, result in results:
            out_ref[:, pl.ds(target, leaf)] += result
        return carry

    lax.fori_loop(0, (count + GROUP - 1) // GROUP, several, 0)


def couple(cells, rows, weights):
    rank = cells.shape[1]
    coefs = jnp.concatenate(
        [row[:, :rank] * weight for row, weight in zip(rows, weights)], axis=1
    )
    partner_cells = jnp.concatenate([row[:, rank:] for row in rows], axis=1)
    sources, _ = distance_factors(partner_cells)
    _, targets = distance_factors(cells)
    tile = decay(product_rows(sources, targets))
    main = tile.astype(BF16)
    rest = (tile - main.astype(F32)).astype(BF16)
    pieces = two_pieces(coefs)
    return fold(product(pieces, main) + product(pieces, rest))


def down_kernel(
    far_ref,
    near_ref,
    basis_ref,
    transfer_ref,
    own_ref,
    left_ref,
    right_ref,
    roots_ref,
    transfer_top_ref,
    skeleton_top_ref,
    out_ref,
    wide_ref,
    top_ref,
    coupled_ref,
    field_ref,
):
    leaf_dev, rank, leaf = basis_ref.shape
    devices = roots_ref.shape[0]
    local = leaf_dev.bit_length() - 1
    top = devices.bit_length() - 1
    rows = leaf_dev - 1
    me = lax.axis_index("dev")

    for part, ref in enumerate((left_ref, own_ref, right_ref)):
        wide_ref[part * rows : (part + 1) * rows] = ref[...]
    top_ref[0:devices] = roots_ref[...]

    def top_row(step, spot):
        if step == 0:
            return spot
        return devices + devices - (devices >> (step - 1)) + spot

    for step in range(1, top):
        first = devices - (devices >> (step - 1))

        def lift(spot, step=step, first=first):
            joined = jnp.concatenate(
                [top_ref[top_row(step - 1, 2 * spot + part)][:, :rank] for part in range(2)],
                axis=1,
            )
            coef = fold(product_across(two_pieces(joined), transfer_top_ref[first + spot]))
            cells = skeleton_cells(skeleton_top_ref[pl.ds(first + spot, 1), :])
            top_ref[top_row(step, spot)] = jnp.concatenate([coef, cells], axis=1)

        loop(devices >> step, 16, lift)

    for level in range(1, local):
        first = level_row(leaf_dev, level)
        count = leaf_dev >> level

        def couple_pair(pair, first=first, count=count):
            halves = []
            for part in range(2):
                spot = pair * 2 + part
                partners, weights = [], []
                for slot in range(far_ref.shape[1]):
                    offset = far_ref[first + spot, slot]
                    partner = spot + offset
                    side = jnp.where(partner < 0, 0, jnp.where(partner < count, 1, 2))
                    partners.append(wide_ref[side * rows + first + partner - (side - 1) * count])
                    weights.append(jnp.where(offset != 0, 1.0, 0.0))
                mine = wide_ref[rows + first + spot]
                halves.append(couple(mine[:, rank:], partners, weights))
            coupled_ref[first // 2 + pair] = jnp.concatenate(halves, axis=1)

        loop(count // 2, 2, couple_pair)

    field = None
    for step in range(top - 1, -1, -1):
        spot = me >> step
        mine = top_ref[top_row(step, spot)]
        sibling = top_ref[top_row(step, spot ^ 1)]
        coupled = couple(mine[:, rank:], [sibling], [1.0])
        if field is None:
            field = coupled
        else:
            parent = devices - (devices >> step) + (spot >> 1)
            both = fold(product(two_pieces(field), transfer_top_ref[parent]))
            field = jnp.where((spot & 1) == 1, both[:, rank:], both[:, :rank]) + coupled

    fields = [field]
    for level in range(local - 1, -1, -1):
        first = level_row(leaf_dev, level + 1)
        below = []
        for spot, parent in enumerate(fields):
            both = fold(product(two_pieces(parent), transfer_ref[first + spot]))
            if level >= 1:
                both = both + coupled_ref[level_row(leaf_dev, level) // 2 + spot]
                below += [both[:, :rank], both[:, rank:]]
            else:
                field_ref[spot] = both
        fields = below

    def expand(pair):
        both = field_ref[pair]
        for part in range(2):
            spot = pair * 2 + part
            pieces = two_pieces(both[:, part * rank : (part + 1) * rank])
            columns = pl.ds(pl.multiple_of(spot * leaf, leaf), leaf)
            out_ref[:, columns] = near_ref[:, columns] + fold(product(pieces, basis_ref[spot]))

    loop(leaf_dev // 2, 4, expand)


def body(
    vectors, points, leaf_basis, near_list, far_list, transfer, skeleton, transfer_top, skeleton_top
):
    rhs, cells = vectors.shape
    leaf_dev, rank, leaf = leaf_basis.shape
    slots = near_list.shape[1]
    devices = lax.axis_size("dev")
    reach = leaf_dev // 2
    wide = leaf_dev + 2 * reach
    rows = leaf_dev - 1
    edge = reach * leaf
    vmem = pl.BlockSpec(memory_space=pltpu.VMEM)
    smem = pl.BlockSpec(memory_space=pltpu.SMEM)
    params = pltpu.CompilerParams(vmem_limit_bytes=VMEM_BYTES)

    ends = devices - 1
    to_right = [(i, i + 1) for i in range(ends)]
    to_left = [(i + 1, i) for i in range(ends)]
    points_left = lax.ppermute(points[:, cells - edge :], "dev", to_right)
    points_right = lax.ppermute(points[:, :edge], "dev", to_left)
    vec_left = lax.ppermute(vectors[:, cells - edge :], "dev", to_right)
    vec_right = lax.ppermute(vectors[:, :edge], "dev", to_left)

    table = pl.pallas_call(
        up_kernel,
        out_shape=jax.ShapeDtypeStruct((rows, rhs, 2 * rank), F32),
        in_specs=[vmem] * 4,
        out_specs=vmem,
        scratch_shapes=[pltpu.VMEM((leaf_dev // 2, rhs, 2 * rank), F32)],
        compiler_params=params,
        cost_estimate=pl.CostEstimate(
            flops=2 * 256 * 256 * 256 * 64, bytes_accessed=4 * 2**20, transcendentals=0
        ),
        name="upward",
    )(vectors, leaf_basis, transfer, skeleton)

    table_left = lax.ppermute(table, "dev", to_right)
    table_right = lax.ppermute(table, "dev", to_left)
    roots = lax.all_gather(table[rows - 1 :], "dev", axis=0, tiled=True)

    tasks = leaf_dev * slots + 2 * GROUP
    near = pl.pallas_call(
        near_kernel,
        out_shape=jax.ShapeDtypeStruct((rhs, cells), F32),
        in_specs=[smem] + [vmem] * 6,
        out_specs=vmem,
        scratch_shapes=[
            pltpu.VMEM((FEATURES, (wide + 1) * leaf), BF16),
            pltpu.VMEM((FEATURES, cells), BF16),
            pltpu.VMEM((rhs, (wide + 1) * leaf), F32),
            pltpu.SMEM((tasks,), jnp.int32),
            pltpu.SMEM((tasks,), jnp.int32),
        ],
        compiler_params=params,
        cost_estimate=pl.CostEstimate(
            flops=2 * 256 * 256 * 256 * 64 * 20, bytes_accessed=2 * 2**20, transcendentals=2**25
        ),
        name="near",
    )(near_list, points, points_left, points_right, vectors, vec_left, vec_right)

    return pl.pallas_call(
        down_kernel,
        out_shape=jax.ShapeDtypeStruct((rhs, cells), F32),
        in_specs=[smem] + [vmem] * 9,
        out_specs=vmem,
        scratch_shapes=[
            pltpu.VMEM((3 * rows, rhs, 2 * rank), F32),
            pltpu.VMEM((2 * devices, rhs, 2 * rank), F32),
            pltpu.VMEM((leaf_dev // 2, rhs, 2 * rank), F32),
            pltpu.VMEM((leaf_dev // 2, rhs, 2 * rank), F32),
        ],
        compiler_params=params,
        cost_estimate=pl.CostEstimate(
            flops=2 * 256 * 256 * 256 * 64, bytes_accessed=4 * 2**20, transcendentals=2**21
        ),
        name="downward",
    )(
        far_list,
        near,
        leaf_basis,
        transfer,
        table,
        table_left,
        table_right,
        roots,
        transfer_top,
        skeleton_top,
    )


def solution(mesh):
    return jax.shard_map(
        body,
        mesh=mesh,
        in_specs=(
            P(None, "dev"),
            P(None, "dev"),
            P("dev", None, None),
            P("dev", None),
            P("dev", None),
            P("dev", None, None),
            P("dev", None),
            P(),
            P(),
        ),
        out_specs=P(None, "dev"),
        check_vma=False,
    )
```

```python
import math

import jax
import jax.numpy as jnp
from jax import lax
from jax.experimental import pallas as pl
from jax.experimental.pallas import tpu as pltpu
from jax.sharding import PartitionSpec as P

F32 = jnp.float32
BF16 = jnp.bfloat16
LOG2E = math.log2(math.e)
TINY = 1e-30
FEATURES = 48
GROUP = 4
STRIP = 128
MESH = pl.DeviceIdType.MESH
VMEM_BYTES = 56 * 1024 * 1024


def loop(count, unroll, step):
    unroll = min(unroll, count)

    def several(index, carry):
        for part in range(unroll):
            step(index * unroll + part)
        return carry

    lax.fori_loop(0, count // unroll, several, 0)


def level_row(leaf_count, level):
    return leaf_count - (leaf_count >> (level - 1))


def three_pieces(values):
    first = values.astype(BF16).astype(F32)
    rest = values - first
    second = rest.astype(BF16).astype(F32)
    return first, second, rest - second


def distance_factors(cells):
    scaled = cells * LOG2E
    norms = jnp.sum(scaled * scaled, axis=0, keepdims=True)
    row = lax.broadcasted_iota(jnp.int32, scaled.shape, 0)
    source = jnp.where(row == 3, norms, jnp.where(row == 4, 1.0, scaled))
    target = jnp.where(row == 3, 1.0, jnp.where(row == 4, norms, -2.0 * scaled))
    s1, s2, s3 = three_pieces(source)
    t1, t2, t3 = three_pieces(target)
    sources = jnp.concatenate([s1, s1, s2, s2, s1, s3], axis=0).astype(BF16)
    targets = jnp.concatenate([t1, t2, t1, t2, t3, t1], axis=0).astype(BF16)
    return sources, targets


def decay(squares):
    kept = jnp.maximum(squares, TINY)
    return jnp.exp2(-(kept * lax.rsqrt(kept)))


def product_rows(left, right):
    return lax.dot_general(left, right, (((0,), (0,)), ((), ())), preferred_element_type=F32)


def product(left, right):
    return lax.dot_general(left, right, (((1,), (0,)), ((), ())), preferred_element_type=F32)


def product_across(left, right):
    return lax.dot_general(left, right, (((1,), (1,)), ((), ())), preferred_element_type=F32)


def two_pieces(values):
    first = values.astype(BF16).astype(F32)
    return jnp.concatenate([first, values - first], axis=0).astype(BF16)


def fold(values):
    half = values.shape[0] // 2
    return values[:half] + values[half:]


def skeleton_cells(row):
    rank = row.shape[1] // 3
    parts = [row[:, c * rank : (c + 1) * rank] for c in range(3)]
    return jnp.concatenate(parts + [jnp.zeros((5, rank), F32)], axis=0)


def up_kernel(
    points_ref,
    vec_ref,
    basis_ref,
    transfer_ref,
    skeleton_ref,
    table_ref,
    table_left_ref,
    table_right_ref,
    roots_ref,
    points_left_ref,
    points_right_ref,
    vec_left_ref,
    vec_right_ref,
    pair_ref,
    send_sem,
    recv_sem,
    root_send_sem,
    root_recv_sem,
    own_sem,
):
    leaf_dev, rank, leaf = basis_ref.shape
    local = leaf_dev.bit_length() - 1
    rows = leaf_dev - 1
    devices = roots_ref.shape[0]
    me = lax.axis_index("dev")
    right = (me + 1) % devices
    left = (me + devices - 1) % devices

    barrier = pltpu.get_barrier_semaphore()

    def greet(shift, carry):
        pl.semaphore_signal(
            barrier, inc=1, device_id=((me + shift) % devices,), device_id_type=MESH
        )
        return carry

    lax.fori_loop(1, devices, greet, 0)
    pl.semaphore_wait(barrier, devices - 1)

    def beside(source, arrival, device, index):
        return pltpu.make_async_remote_copy(
            src_ref=source,
            dst_ref=arrival,
            send_sem=send_sem.at[index],
            recv_sem=recv_sem.at[index],
            device_id=(device,),
            device_id_type=MESH,
        )

    leaf_copies = [
        beside(points_ref, points_left_ref, right, 0),
        beside(points_ref, points_right_ref, left, 1),
        beside(vec_ref, vec_left_ref, right, 2),
        beside(vec_ref, vec_right_ref, left, 3),
    ]
    for copy in leaf_copies:
        copy.start()

    def leaf_pair(pair):
        halves = []
        for part in range(2):
            spot = pair * 2 + part
            own = vec_ref[:, pl.ds(pl.multiple_of(spot * leaf, leaf), leaf)]
            halves.append(product_across(own, basis_ref[spot]))
        pair_ref[pair] = jnp.concatenate(halves, axis=1)

    loop(leaf_dev // 2, 8, leaf_pair)
    joined = [pair_ref[pair] for pair in range(leaf_dev // 2)]
    for level in range(1, local + 1):
        first = level_row(leaf_dev, level)
        coefs = []
        for spot in range(leaf_dev >> level):
            coef = fold(product_across(two_pieces(joined[spot]), transfer_ref[first + spot]))
            cells = skeleton_cells(skeleton_ref[pl.ds(first + spot, 1), :])
            table_ref[first + spot] = jnp.concatenate([coef, cells], axis=1)
            coefs.append(coef)
        joined = [
            jnp.concatenate(coefs[2 * spot : 2 * spot + 2], axis=1)
            for spot in range(len(coefs) // 2)
        ]

    root = table_ref.at[pl.ds(rows - 1, 1)]
    mine = roots_ref.at[pl.ds(me, 1)]

    def root_copy(shift):
        return pltpu.make_async_remote_copy(
            src_ref=root,
            dst_ref=mine,
            send_sem=root_send_sem.at[shift],
            recv_sem=root_recv_sem.at[shift],
            device_id=((me + shift) % devices,),
            device_id_type=MESH,
        )

    def send_root(shift, carry):
        root_copy(shift).start()
        return carry

    def wait_root(shift, carry):
        root_copy(shift).wait()
        return carry

    table_copies = [
        beside(table_ref, table_left_ref, right, 4),
        beside(table_ref, table_right_ref, left, 5),
    ]
    for copy in table_copies:
        copy.start()
    lax.fori_loop(1, devices, send_root, 0)
    own_copy = pltpu.make_async_copy(root, mine, own_sem)
    own_copy.start()
    for copy in leaf_copies + table_copies:
        copy.wait()
    lax.fori_loop(1, devices, wait_root, 0)
    own_copy.wait()


def near_kernel(
    list_ref,
    points_ref,
    points_left_ref,
    points_right_ref,
    vec_ref,
    vec_left_ref,
    vec_right_ref,
    out_ref,
    source_ref,
    target_ref,
    wide_vec_ref,
    task_target_ref,
    task_source_ref,
):
    slots, leaf_dev = list_ref.shape
    leaf = points_ref.shape[1] // leaf_dev
    reach = leaf_dev // 2
    wide = leaf_dev + 2 * reach
    chunk = 4 * leaf

    def cells_of(ref, start):
        part = ref[:, pl.ds(start, chunk)]
        return jnp.concatenate([part, jnp.zeros((5, chunk), F32)], axis=0)

    def fill(points, vecs, base, first, length, own):
        def step(index):
            start = pl.multiple_of(first + index * chunk, chunk)
            spot = pl.multiple_of(base + index * chunk, chunk)
            sources, targets = distance_factors(cells_of(points, start))
            source_ref[:, pl.ds(spot, chunk)] = sources
            if own:
                target_ref[:, pl.ds(start, chunk)] = targets
                out_ref[:, pl.ds(start, chunk)] = jnp.zeros((out_ref.shape[0], chunk), F32)
            wide_vec_ref[:, pl.ds(spot, chunk)] = vecs[:, pl.ds(start, chunk)].astype(F32)

        loop(length // chunk, 2, step)

    edge = reach * leaf
    cells = leaf_dev * leaf
    fill(points_left_ref, vec_left_ref, 0, cells - edge, edge, False)
    fill(points_ref, vec_ref, edge, 0, cells, True)
    fill(points_right_ref, vec_right_ref, edge + cells, 0, edge, False)
    empty = pl.ds(wide * leaf, leaf)
    source_ref[:, empty] = jnp.zeros((FEATURES, leaf), BF16)
    wide_vec_ref[:, empty] = jnp.zeros((wide_vec_ref.shape[0], leaf), F32)

    def enlist(target, count):
        for slot in range(slots):
            offset = list_ref[slot, target]
            task_target_ref[count] = target
            task_source_ref[count] = target + offset + reach
            if slot == 0:
                count = count + 1
            else:
                count = count + jnp.where(offset != 0, 1, 0)
        return count

    count = lax.fori_loop(0, leaf_dev, enlist, 0)
    for extra in range(GROUP):
        task_target_ref[count + extra] = 0
        task_source_ref[count + extra] = wide

    def several(index, carry):
        results = []
        for part in range(GROUP):
            target = pl.multiple_of(task_target_ref[index * GROUP + part] * leaf, leaf)
            source = pl.multiple_of(task_source_ref[index * GROUP + part] * leaf, leaf)
            sources = source_ref[:, pl.ds(source, leaf)]
            targets = target_ref[:, pl.ds(target, leaf)]
            tile = jnp.concatenate(
                [
                    decay(product_rows(sources[:, start : start + STRIP], targets)).astype(BF16)
                    for start in range(0, leaf, STRIP)
                ],
                axis=0,
            )
            vec = wide_vec_ref[:, pl.ds(source, leaf)].astype(BF16)
            results.append((target, product(vec, tile)))
        for target, result in results:
            out_ref[:, pl.ds(target, leaf)] += result
        return carry

    lax.fori_loop(0, (count + GROUP - 1) // GROUP, several, 0)


def couple(cells, rows, weights):
    rank = cells.shape[1]
    coefs = jnp.concatenate(
        [row[:, :rank] * weight for row, weight in zip(rows, weights)], axis=1
    )
    partner_cells = jnp.concatenate([row[:, rank:] for row in rows], axis=1)
    sources, _ = distance_factors(partner_cells)
    _, targets = distance_factors(cells)
    tile = decay(product_rows(sources, targets))
    main = tile.astype(BF16)
    rest = (tile - main.astype(F32)).astype(BF16)
    pieces = two_pieces(coefs)
    return fold(product(pieces, main) + product(pieces, rest))


def down_kernel(
    far_ref,
    near_ref,
    basis_ref,
    transfer_ref,
    own_ref,
    left_ref,
    right_ref,
    roots_ref,
    transfer_top_ref,
    skeleton_top_ref,
    out_ref,
    wide_ref,
    top_ref,
    coupled_ref,
    field_ref,
):
    leaf_dev, rank, leaf = basis_ref.shape
    devices = roots_ref.shape[0]
    local = leaf_dev.bit_length() - 1
    top = devices.bit_length() - 1
    rows = leaf_dev - 1
    me = lax.axis_index("dev")

    for part, ref in enumerate((left_ref, own_ref, right_ref)):
        wide_ref[part * rows : (part + 1) * rows] = ref[...]
    top_ref[0:devices] = roots_ref[...]

    def top_row(step, spot):
        if step == 0:
            return spot
        return devices + devices - (devices >> (step - 1)) + spot

    for step in range(1, top):
        first = devices - (devices >> (step - 1))

        def lift(spot, step=step, first=first):
            joined = jnp.concatenate(
                [top_ref[top_row(step - 1, 2 * spot + part)][:, :rank] for part in range(2)],
                axis=1,
            )
            coef = fold(product_across(two_pieces(joined), transfer_top_ref[first + spot]))
            cells = skeleton_cells(skeleton_top_ref[pl.ds(first + spot, 1), :])
            top_ref[top_row(step, spot)] = jnp.concatenate([coef, cells], axis=1)

        loop(devices >> step, 16, lift)

    for level in range(1, local):
        first = level_row(leaf_dev, level)
        count = leaf_dev >> level

        def couple_pair(pair, first=first, count=count):
            halves = []
            for part in range(2):
                spot = pair * 2 + part
                partners, weights = [], []
                for slot in range(far_ref.shape[0]):
                    offset = far_ref[slot, first + spot]
                    partner = spot + offset
                    side = jnp.where(partner < 0, 0, jnp.where(partner < count, 1, 2))
                    partners.append(wide_ref[side * rows + first + partner - (side - 1) * count])
                    weights.append(jnp.where(offset != 0, 1.0, 0.0))
                mine = wide_ref[rows + first + spot]
                halves.append(couple(mine[:, rank:], partners, weights))
            coupled_ref[first // 2 + pair] = jnp.concatenate(halves, axis=1)

        loop(count // 2, 4, couple_pair)

    field = None
    for step in range(top - 1, -1, -1):
        spot = me >> step
        mine = top_ref[top_row(step, spot)]
        sibling = top_ref[top_row(step, spot ^ 1)]
        coupled = couple(mine[:, rank:], [sibling], [1.0])
        if field is None:
            field = coupled
        else:
            parent = devices - (devices >> step) + (spot >> 1)
            both = fold(product(two_pieces(field), transfer_top_ref[parent]))
            field = jnp.where((spot & 1) == 1, both[:, rank:], both[:, :rank]) + coupled

    fields = [field]
    for level in range(local - 1, -1, -1):
        first = level_row(leaf_dev, level + 1)
        below = []
        for spot, parent in enumerate(fields):
            both = fold(product(two_pieces(parent), transfer_ref[first + spot]))
            if level >= 1:
                both = both + coupled_ref[level_row(leaf_dev, level) // 2 + spot]
                below += [both[:, :rank], both[:, rank:]]
            else:
                field_ref[spot] = both
        fields = below

    def expand(pair):
        both = field_ref[pair]
        for part in range(2):
            spot = pair * 2 + part
            pieces = two_pieces(both[:, part * rank : (part + 1) * rank])
            columns = pl.ds(pl.multiple_of(spot * leaf, leaf), leaf)
            out_ref[:, columns] = near_ref[:, columns] + fold(product(pieces, basis_ref[spot]))

    loop(leaf_dev // 2, 4, expand)


def body(
    vectors, points, leaf_basis, near_list, far_list, transfer, skeleton, transfer_top, skeleton_top
):
    rhs, cells = vectors.shape
    leaf_dev, rank, leaf = leaf_basis.shape
    slots = near_list.shape[1]
    devices = lax.axis_size("dev")
    wide = 2 * leaf_dev
    rows = leaf_dev - 1
    vmem = pl.BlockSpec(memory_space=pltpu.VMEM)
    smem = pl.BlockSpec(memory_space=pltpu.SMEM)
    hbm = pl.BlockSpec(memory_space=pl.ANY)
    params = pltpu.CompilerParams(vmem_limit_bytes=VMEM_BYTES)

    table_shape = jax.ShapeDtypeStruct((rows, rhs, 2 * rank), F32)
    points_shape = jax.ShapeDtypeStruct(points.shape, points.dtype)
    vec_shape = jax.ShapeDtypeStruct(vectors.shape, vectors.dtype)
    (
        table,
        table_left,
        table_right,
        roots,
        points_left,
        points_right,
        vec_left,
        vec_right,
    ) = pl.pallas_call(
        up_kernel,
        out_shape=(
            table_shape,
            table_shape,
            table_shape,
            jax.ShapeDtypeStruct((devices, rhs, 2 * rank), F32),
            points_shape,
            points_shape,
            vec_shape,
            vec_shape,
        ),
        in_specs=[vmem] * 5,
        out_specs=(vmem,) + (hbm,) * 7,
        scratch_shapes=[
            pltpu.VMEM((leaf_dev // 2, rhs, 2 * rank), F32),
            pltpu.SemaphoreType.DMA((6,)),
            pltpu.SemaphoreType.DMA((6,)),
            pltpu.SemaphoreType.DMA((devices,)),
            pltpu.SemaphoreType.DMA((devices,)),
            pltpu.SemaphoreType.DMA,
        ],
        compiler_params=pltpu.CompilerParams(
            vmem_limit_bytes=VMEM_BYTES, collective_id=0, has_side_effects=True
        ),
        cost_estimate=pl.CostEstimate(
            flops=2 * 256 * 256 * 256 * 64, bytes_accessed=4 * 2**20, transcendentals=0
        ),
        name="upward",
    )(points, vectors, leaf_basis, transfer, skeleton)

    tasks = leaf_dev * slots + 2 * GROUP
    near = pl.pallas_call(
        near_kernel,
        out_shape=jax.ShapeDtypeStruct((rhs, cells), F32),
        in_specs=[smem] + [vmem] * 6,
        out_specs=vmem,
        scratch_shapes=[
            pltpu.VMEM((FEATURES, (wide + 1) * leaf), BF16),
            pltpu.VMEM((FEATURES, cells), BF16),
            pltpu.VMEM((rhs, (wide + 1) * leaf), F32),
            pltpu.SMEM((tasks,), jnp.int32),
            pltpu.SMEM((tasks,), jnp.int32),
        ],
        compiler_params=params,
        cost_estimate=pl.CostEstimate(
            flops=2 * 256 * 256 * 256 * 64 * 20, bytes_accessed=2 * 2**20, transcendentals=2**25
        ),
        name="near",
    )(near_list.T, points, points_left, points_right, vectors, vec_left, vec_right)

    return pl.pallas_call(
        down_kernel,
        out_shape=jax.ShapeDtypeStruct((rhs, cells), F32),
        in_specs=[smem] + [vmem] * 9,
        out_specs=vmem,
        scratch_shapes=[
            pltpu.VMEM((3 * rows, rhs, 2 * rank), F32),
            pltpu.VMEM((2 * devices, rhs, 2 * rank), F32),
            pltpu.VMEM((leaf_dev // 2, rhs, 2 * rank), F32),
            pltpu.VMEM((leaf_dev // 2, rhs, 2 * rank), F32),
        ],
        compiler_params=params,
        cost_estimate=pl.CostEstimate(
            flops=2 * 256 * 256 * 256 * 64, bytes_accessed=4 * 2**20, transcendentals=2**21
        ),
        name="downward",
    )(
        far_list.T,
        near,
        leaf_basis,
        transfer,
        table,
        table_left,
        table_right,
        roots,
        transfer_top,
        skeleton_top,
    )


def solution(mesh):
    return jax.shard_map(
        body,
        mesh=mesh,
        in_specs=(
            P(None, "dev"),
            P(None, "dev"),
            P("dev", None, None),
            P("dev", None),
            P("dev", None),
            P("dev", None, None),
            P("dev", None),
            P(),
            P(),
        ),
        out_specs=P(None, "dev"),
        check_vma=False,
    )
```

```python
import math

import jax
import jax.numpy as jnp
from jax import lax
from jax.experimental import pallas as pl
from jax.experimental.pallas import tpu as pltpu
from jax.sharding import PartitionSpec as P

F32 = jnp.float32
BF16 = jnp.bfloat16
LOG2E = math.log2(math.e)
TINY = 1e-30
FEATURES = 48
GROUP = 4
STRIP = 128
MESH = pl.DeviceIdType.MESH
VMEM_BYTES = 56 * 1024 * 1024


def loop(count, unroll, step):
    unroll = min(unroll, count)

    def several(index, carry):
        for part in range(unroll):
            step(index * unroll + part)
        return carry

    lax.fori_loop(0, count // unroll, several, 0)


def level_row(leaf_count, level):
    return leaf_count - (leaf_count >> (level - 1))


def three_pieces(values):
    first = values.astype(BF16).astype(F32)
    rest = values - first
    second = rest.astype(BF16).astype(F32)
    return first, second, rest - second


def distance_factors(cells):
    row = lax.broadcasted_iota(jnp.int32, cells.shape, 0)
    scaled = jnp.where(row < 3, cells * LOG2E, 0.0)
    norms = jnp.sum(scaled * scaled, axis=0, keepdims=True)
    source = jnp.where(row == 3, norms, jnp.where(row == 4, 1.0, scaled))
    target = jnp.where(row == 3, 1.0, jnp.where(row == 4, norms, -2.0 * scaled))
    s1, s2, s3 = three_pieces(source)
    t1, t2, t3 = three_pieces(target)
    sources = jnp.concatenate([s1, s1, s2, s2, s1, s3], axis=0).astype(BF16)
    targets = jnp.concatenate([t1, t2, t1, t2, t3, t1], axis=0).astype(BF16)
    return sources, targets


def decay(squares):
    kept = jnp.maximum(squares, TINY)
    return jnp.exp2(-(kept * lax.rsqrt(kept)))


def product_rows(left, right):
    return lax.dot_general(left, right, (((0,), (0,)), ((), ())), preferred_element_type=F32)


def product(left, right):
    return lax.dot_general(left, right, (((1,), (0,)), ((), ())), preferred_element_type=F32)


def product_across(left, right):
    return lax.dot_general(left, right, (((1,), (1,)), ((), ())), preferred_element_type=F32)


def two_pieces(values):
    first = values.astype(BF16).astype(F32)
    return jnp.concatenate([first, values - first], axis=0).astype(BF16)


def fold(values):
    half = values.shape[0] // 2
    return values[:half] + values[half:]


def skeleton_cells(row):
    rank = row.shape[1] // 3
    parts = [row[:, c * rank : (c + 1) * rank] for c in range(3)]
    return jnp.concatenate(parts + [jnp.zeros((5, rank), F32)], axis=0)


def task_cells(offsets, rank):
    slots, leaf_dev = offsets.shape
    slot = lax.broadcasted_iota(jnp.int32, offsets.shape, 0)
    spot = lax.broadcasted_iota(jnp.int32, offsets.shape, 1)
    used = jnp.where((slot == 0) | (offsets != 0), 1.0, 0.0)
    lower = jnp.sum(jnp.where(spot < leaf_dev // 2, used, 0.0), keepdims=True)
    upper = jnp.sum(jnp.where(spot < leaf_dev // 2, 0.0, used), keepdims=True)
    row = lax.broadcasted_iota(jnp.int32, (8, rank), 0)
    column = lax.broadcasted_iota(jnp.int32, (8, rank), 1)
    counts = jnp.where(column == 0, lower, jnp.where(column == 1, upper, 0.0))
    return jnp.where(row == 5, counts, 0.0)


def up_kernel(
    list_ref,
    points_ref,
    vec_ref,
    basis_ref,
    transfer_ref,
    skeleton_ref,
    table_ref,
    table_left_ref,
    table_right_ref,
    roots_ref,
    points_left_ref,
    points_right_ref,
    vec_left_ref,
    vec_right_ref,
    list_left_ref,
    list_right_ref,
    pair_ref,
    send_sem,
    recv_sem,
    root_send_sem,
    root_recv_sem,
    own_sem,
):
    leaf_dev, rank, leaf = basis_ref.shape
    local = leaf_dev.bit_length() - 1
    rows = leaf_dev - 1
    devices = roots_ref.shape[0]
    me = lax.axis_index("dev")
    right = (me + 1) % devices
    left = (me + devices - 1) % devices
    has_right = me < devices - 1
    has_left = me > 0

    barrier = pltpu.get_barrier_semaphore()

    def greet(shift, carry):
        pl.semaphore_signal(
            barrier, inc=1, device_id=((me + shift) % devices,), device_id_type=MESH
        )
        return carry

    lax.fori_loop(1, devices, greet, 0)
    pl.semaphore_wait(barrier, devices - 1)

    def beside(source, arrival, device, index):
        return pltpu.make_async_remote_copy(
            src_ref=source,
            dst_ref=arrival,
            send_sem=send_sem.at[index],
            recv_sem=recv_sem.at[index],
            device_id=(device,),
            device_id_type=MESH,
        )

    leaf_right = [
        beside(points_ref, points_left_ref, right, 0),
        beside(vec_ref, vec_left_ref, right, 1),
        beside(list_ref, list_left_ref, right, 2),
    ]
    leaf_left = [
        beside(points_ref, points_right_ref, left, 3),
        beside(vec_ref, vec_right_ref, left, 4),
        beside(list_ref, list_right_ref, left, 5),
    ]
    table_right = beside(table_ref, table_left_ref, right, 6)
    table_left = beside(table_ref, table_right_ref, left, 7)

    @pl.when(has_right)
    def _():
        for copy in leaf_right:
            copy.start()

    @pl.when(has_left)
    def _():
        for copy in leaf_left:
            copy.start()

    def leaf_pair(pair):
        halves = []
        for part in range(2):
            spot = pair * 2 + part
            own = vec_ref[:, pl.ds(pl.multiple_of(spot * leaf, leaf), leaf)]
            halves.append(product_across(own, basis_ref[spot]))
        pair_ref[pair] = jnp.concatenate(halves, axis=1)

    loop(leaf_dev // 2, 8, leaf_pair)
    joined = [pair_ref[pair] for pair in range(leaf_dev // 2)]
    for level in range(1, local + 1):
        first = level_row(leaf_dev, level)
        coefs = []
        for spot in range(leaf_dev >> level):
            coef = fold(product_across(two_pieces(joined[spot]), transfer_ref[first + spot]))
            cells = skeleton_cells(skeleton_ref[pl.ds(first + spot, 1), :])
            if level == local:
                cells = cells + task_cells(list_ref[...], rank)
            table_ref[first + spot] = jnp.concatenate([coef, cells], axis=1)
            coefs.append(coef)
        joined = [
            jnp.concatenate(coefs[2 * spot : 2 * spot + 2], axis=1)
            for spot in range(len(coefs) // 2)
        ]

    root = table_ref.at[pl.ds(rows - 1, 1)]
    mine = roots_ref.at[pl.ds(me, 1)]

    def root_copy(shift):
        return pltpu.make_async_remote_copy(
            src_ref=root,
            dst_ref=mine,
            send_sem=root_send_sem.at[shift],
            recv_sem=root_recv_sem.at[shift],
            device_id=((me + shift) % devices,),
            device_id_type=MESH,
        )

    def send_root(shift, carry):
        root_copy(shift).start()
        return carry

    def wait_root(shift, carry):
        root_copy(shift).wait()
        return carry

    @pl.when(has_right)
    def _():
        table_right.start()

    @pl.when(has_left)
    def _():
        table_left.start()

    lax.fori_loop(1, devices, send_root, 0)
    own_copy = pltpu.make_async_copy(root, mine, own_sem)
    own_copy.start()

    @pl.when(has_right)
    def _():
        for copy in leaf_right + [table_right]:
            copy.wait_send()
        for copy in leaf_left + [table_left]:
            copy.wait_recv()

    @pl.when(has_left)
    def _():
        for copy in leaf_left + [table_left]:
            copy.wait_send()
        for copy in leaf_right + [table_right]:
            copy.wait_recv()

    lax.fori_loop(1, devices, wait_root, 0)
    own_copy.wait()


def balance(counts_ref, me):
    devices = counts_ref.shape[0]

    def total_and_most(spot, carry):
        total, most = carry
        own = counts_ref[spot, 0] + counts_ref[spot, 1]
        return total + own, jnp.maximum(most, own)

    total, most = lax.fori_loop(0, devices, total_and_most, (0, 0))

    def hand(spot, flow, limit):
        own = counts_ref[spot, 0] + counts_ref[spot, 1]
        after = jnp.minimum(spot + 1, devices - 1)
        lower = jnp.where(spot + 1 < devices, counts_ref[after, 0], 0)
        upper = jnp.where(spot + 1 < devices, counts_ref[spot, 1], 0)
        flow = jnp.maximum(own + flow - limit, -lower)
        return flow, jnp.where(flow <= upper, 1, 0)

    def halve(step, carry):
        low, high = carry
        limit = (low + high) >> 1

        def walk(spot, state):
            flow, fits = state
            flow, here = hand(spot, flow, limit)
            return flow, fits & here

        _, fits = lax.fori_loop(0, devices, walk, (0, 1))
        return jnp.where(fits == 1, low, limit + 1), jnp.where(fits == 1, limit, high)

    _, limit = lax.fori_loop(0, 6, halve, (total >> (devices.bit_length() - 1), most))
    before = lax.fori_loop(0, me, lambda spot, flow: hand(spot, flow, limit)[0], 0)
    return before, hand(me, before, limit)[0]


def near_kernel(
    counts_ref,
    list_ref,
    list_left_ref,
    list_right_ref,
    points_ref,
    points_left_ref,
    points_right_ref,
    vec_ref,
    vec_left_ref,
    vec_right_ref,
    out_ref,
    source_ref,
    target_ref,
    wide_vec_ref,
    task_target_ref,
    task_source_ref,
):
    slots, leaf_dev = list_ref.shape
    leaf = points_ref.shape[1] // leaf_dev
    half = leaf_dev // 2
    cells = leaf_dev * leaf
    edge = half * leaf
    wide = 3 * leaf_dev
    chunk = 4 * leaf
    me = lax.axis_index("dev")

    def fill(points, vecs, base, first, length, aimed):
        def step(index):
            start = pl.multiple_of(first + index * chunk, chunk)
            spot = pl.multiple_of(base + start, chunk)
            part = points[:, pl.ds(start, chunk)]
            part = jnp.concatenate([part, jnp.zeros((5, chunk), F32)], axis=0)
            sources, targets = distance_factors(part)
            source_ref[:, pl.ds(spot, chunk)] = sources
            if aimed:
                aim = pl.ds(pl.multiple_of(spot - edge, chunk), chunk)
                target_ref[:, aim] = targets
                out_ref[:, aim] = jnp.zeros((out_ref.shape[0], chunk), F32)
            wide_vec_ref[:, pl.ds(spot, chunk)] = vecs[:, pl.ds(start, chunk)].astype(F32)

        loop(length // chunk, 2, step)

    fill(points_left_ref, vec_left_ref, 0, 0, edge, False)
    fill(points_left_ref, vec_left_ref, 0, edge, edge, True)
    fill(points_ref, vec_ref, cells, 0, cells, True)
    fill(points_right_ref, vec_right_ref, 2 * cells, 0, edge, True)
    fill(points_right_ref, vec_right_ref, 2 * cells, edge, edge, False)
    empty = pl.ds(wide * leaf, leaf)
    source_ref[:, empty] = jnp.zeros((FEATURES, leaf), BF16)
    wide_vec_ref[:, empty] = jnp.zeros((wide_vec_ref.shape[0], leaf), F32)

    before, after = balance(counts_ref, me)

    def enlist(lists, base, first, last, low, high, count):
        def step(spot, carry):
            order, count = carry
            for slot in range(slots):
                offset = lists[slot, spot]
                task_target_ref[count] = base + spot - half
                task_source_ref[count] = base + spot + offset
                used = 1 if slot == 0 else jnp.where(offset != 0, 1, 0)
                kept = jnp.where((order >= low) & (order < high), used, 0)
                order = order + used
                count = count + kept
            return order, count

        return lax.fori_loop(first, last, step, (0, count))[1]

    before_upper = counts_ref[jnp.maximum(me - 1, 0), 1]
    own_tasks = counts_ref[me, 0] + counts_ref[me, 1]
    count = enlist(
        list_ref,
        leaf_dev,
        0,
        leaf_dev,
        jnp.maximum(-before, 0),
        own_tasks - jnp.maximum(after, 0),
        0,
    )
    count = enlist(
        list_left_ref,
        0,
        jnp.where(before > 0, half, leaf_dev),
        leaf_dev,
        before_upper - before,
        before_upper,
        count,
    )
    count = enlist(
        list_right_ref, 2 * leaf_dev, 0, jnp.where(after < 0, half, 0), 0, -after, count
    )
    for extra in range(GROUP):
        task_target_ref[count + extra] = 0
        task_source_ref[count + extra] = wide

    def several(index, carry):
        results = []
        for part in range(GROUP):
            target = pl.multiple_of(task_target_ref[index * GROUP + part] * leaf, leaf)
            source = pl.multiple_of(task_source_ref[index * GROUP + part] * leaf, leaf)
            sources = source_ref[:, pl.ds(source, leaf)]
            targets = target_ref[:, pl.ds(target, leaf)]
            tile = jnp.concatenate(
                [
                    decay(product_rows(sources[:, start : start + STRIP], targets)).astype(BF16)
                    for start in range(0, leaf, STRIP)
                ],
                axis=0,
            )
            vec = wide_vec_ref[:, pl.ds(source, leaf)].astype(BF16)
            results.append((target, product(vec, tile)))
        for target, result in results:
            out_ref[:, pl.ds(target, leaf)] += result
        return carry

    lax.fori_loop(0, (count + GROUP - 1) // GROUP, several, 0)


def couple(cells, rows, weights):
    rank = cells.shape[1]
    coefs = jnp.concatenate(
        [row[:, :rank] * weight for row, weight in zip(rows, weights)], axis=1
    )
    partner_cells = jnp.concatenate([row[:, rank:] for row in rows], axis=1)
    sources, _ = distance_factors(partner_cells)
    _, targets = distance_factors(cells)
    tile = decay(product_rows(sources, targets))
    main = tile.astype(BF16)
    rest = (tile - main.astype(F32)).astype(BF16)
    pieces = two_pieces(coefs)
    return fold(product(pieces, main) + product(pieces, rest))


def down_kernel(
    far_ref,
    near_ref,
    basis_ref,
    transfer_ref,
    own_ref,
    left_ref,
    right_ref,
    roots_ref,
    transfer_top_ref,
    skeleton_top_ref,
    out_ref,
    wide_ref,
    top_ref,
    coupled_ref,
    field_ref,
    help_ref,
    send_sem,
    recv_sem,
):
    leaf_dev, rank, leaf = basis_ref.shape
    devices = roots_ref.shape[0]
    local = leaf_dev.bit_length() - 1
    top = devices.bit_length() - 1
    rows = leaf_dev - 1
    me = lax.axis_index("dev")
    half = leaf_dev // 2
    edge = half * leaf
    has_right = me < devices - 1
    has_left = me > 0
    right = (me + 1) % devices
    left = (me + devices - 1) % devices

    barrier = pltpu.get_barrier_semaphore()

    @pl.when(has_right)
    def _():
        pl.semaphore_signal(barrier, inc=1, device_id=(right,), device_id_type=MESH)

    @pl.when(has_left)
    def _():
        pl.semaphore_signal(barrier, inc=1, device_id=(left,), device_id_type=MESH)

    pl.semaphore_wait(barrier, jnp.where(has_right, 1, 0) + jnp.where(has_left, 1, 0))

    def handed_back(start, index, device):
        return pltpu.make_async_remote_copy(
            src_ref=near_ref.at[:, pl.ds(start, edge)],
            dst_ref=help_ref.at[index],
            send_sem=send_sem.at[index],
            recv_sem=recv_sem.at[index],
            device_id=(device,),
            device_id_type=MESH,
        )

    to_right = handed_back(edge + leaf_dev * leaf, 0, right)
    to_left = handed_back(0, 1, left)

    @pl.when(has_right)
    def _():
        to_right.start()

    @pl.when(has_left)
    def _():
        to_left.start()

    for part, ref in enumerate((left_ref, own_ref, right_ref)):
        wide_ref[part * rows : (part + 1) * rows] = ref[...]
    top_ref[0:devices] = roots_ref[...]

    def top_row(step, spot):
        if step == 0:
            return spot
        return devices + devices - (devices >> (step - 1)) + spot

    for step in range(1, top):
        first = devices - (devices >> (step - 1))

        def lift(spot, step=step, first=first):
            joined = jnp.concatenate(
                [top_ref[top_row(step - 1, 2 * spot + part)][:, :rank] for part in range(2)],
                axis=1,
            )
            coef = fold(product_across(two_pieces(joined), transfer_top_ref[first + spot]))
            cells = skeleton_cells(skeleton_top_ref[pl.ds(first + spot, 1), :])
            top_ref[top_row(step, spot)] = jnp.concatenate([coef, cells], axis=1)

        loop(devices >> step, 16, lift)

    for level in range(1, local):
        first = level_row(leaf_dev, level)
        count = leaf_dev >> level

        def couple_pair(pair, first=first, count=count):
            halves = []
            for part in range(2):
                spot = pair * 2 + part
                partners, weights = [], []
                for slot in range(far_ref.shape[0]):
                    offset = far_ref[slot, first + spot]
                    partner = spot + offset
                    side = jnp.where(partner < 0, 0, jnp.where(partner < count, 1, 2))
                    partners.append(wide_ref[side * rows + first + partner - (side - 1) * count])
                    weights.append(jnp.where(offset != 0, 1.0, 0.0))
                mine = wide_ref[rows + first + spot]
                halves.append(couple(mine[:, rank:], partners, weights))
            coupled_ref[first // 2 + pair] = jnp.concatenate(halves, axis=1)

        loop(count // 2, 4, couple_pair)

    field = None
    for step in range(top - 1, -1, -1):
        spot = me >> step
        mine = top_ref[top_row(step, spot)]
        sibling = top_ref[top_row(step, spot ^ 1)]
        coupled = couple(mine[:, rank:], [sibling], [1.0])
        if field is None:
            field = coupled
        else:
            parent = devices - (devices >> step) + (spot >> 1)
            both = fold(product(two_pieces(field), transfer_top_ref[parent]))
            field = jnp.where((spot & 1) == 1, both[:, rank:], both[:, :rank]) + coupled

    fields = [field]
    for level in range(local - 1, -1, -1):
        first = level_row(leaf_dev, level + 1)
        below = []
        for spot, parent in enumerate(fields):
            both = fold(product(two_pieces(parent), transfer_ref[first + spot]))
            if level >= 1:
                both = both + coupled_ref[level_row(leaf_dev, level) // 2 + spot]
                below += [both[:, :rank], both[:, rank:]]
            else:
                field_ref[spot] = both
        fields = below

    @pl.when(has_right)
    def _():
        to_right.wait_send()
        to_left.wait_recv()

    @pl.when(has_left)
    def _():
        to_left.wait_send()
        to_right.wait_recv()

    @pl.when(jnp.logical_not(has_left))
    def _():
        help_ref[0] = jnp.zeros((help_ref.shape[1], edge), F32)

    @pl.when(jnp.logical_not(has_right))
    def _():
        help_ref[1] = jnp.zeros((help_ref.shape[1], edge), F32)

    for side in range(2):

        def expand(pair, side=side):
            both = field_ref[side * (half // 2) + pair]
            for part in range(2):
                spot = pair * 2 + part
                pieces = two_pieces(both[:, part * rank : (part + 1) * rank])
                inner = pl.multiple_of(spot * leaf, leaf)
                here = pl.multiple_of(side * edge + spot * leaf, leaf)
                there = pl.multiple_of(edge + side * edge + spot * leaf, leaf)
                near = near_ref[:, pl.ds(there, leaf)] + help_ref[side, :, pl.ds(inner, leaf)]
                far = fold(product(pieces, basis_ref[side * half + spot]))
                out_ref[:, pl.ds(here, leaf)] = near + far

        loop(half // 2, 4, expand)


def body(
    vectors, points, leaf_basis, near_list, far_list, transfer, skeleton, transfer_top, skeleton_top
):
    rhs, cells = vectors.shape
    leaf_dev, rank, leaf = leaf_basis.shape
    slots = near_list.shape[1]
    devices = lax.axis_size("dev")
    wide = 3 * leaf_dev
    edge = cells // 2
    rows = leaf_dev - 1
    vmem = pl.BlockSpec(memory_space=pltpu.VMEM)
    smem = pl.BlockSpec(memory_space=pltpu.SMEM)
    hbm = pl.BlockSpec(memory_space=pl.ANY)
    params = pltpu.CompilerParams(vmem_limit_bytes=VMEM_BYTES)

    table_shape = jax.ShapeDtypeStruct((rows, rhs, 2 * rank), F32)
    points_shape = jax.ShapeDtypeStruct(points.shape, points.dtype)
    lists = near_list.T
    list_shape = jax.ShapeDtypeStruct(lists.shape, lists.dtype)
    vec_shape = jax.ShapeDtypeStruct(vectors.shape, vectors.dtype)
    (
        table,
        table_left,
        table_right,
        roots,
        points_left,
        points_right,
        vec_left,
        vec_right,
        list_left,
        list_right,
    ) = pl.pallas_call(
        up_kernel,
        out_shape=(
            table_shape,
            table_shape,
            table_shape,
            jax.ShapeDtypeStruct((devices, rhs, 2 * rank), F32),
            points_shape,
            points_shape,
            vec_shape,
            vec_shape,
            list_shape,
            list_shape,
        ),
        in_specs=[vmem] * 6,
        out_specs=(vmem,) + (hbm,) * 9,
        scratch_shapes=[
            pltpu.VMEM((leaf_dev // 2, rhs, 2 * rank), F32),
            pltpu.SemaphoreType.DMA((8,)),
            pltpu.SemaphoreType.DMA((8,)),
            pltpu.SemaphoreType.DMA((devices,)),
            pltpu.SemaphoreType.DMA((devices,)),
            pltpu.SemaphoreType.DMA,
        ],
        compiler_params=pltpu.CompilerParams(
            vmem_limit_bytes=VMEM_BYTES, collective_id=0, has_side_effects=True
        ),
        cost_estimate=pl.CostEstimate(
            flops=2 * 256 * 256 * 256 * 64, bytes_accessed=4 * 2**20, transcendentals=0
        ),
        name="upward",
    )(lists, points, vectors, leaf_basis, transfer, skeleton)
    counts = roots[:, 5, rank : rank + 2].astype(jnp.int32)

    tasks = 2 * leaf_dev * slots + 2 * GROUP
    near = pl.pallas_call(
        near_kernel,
        out_shape=jax.ShapeDtypeStruct((rhs, cells + 2 * edge), F32),
        in_specs=[smem] * 4 + [vmem] * 6,
        out_specs=vmem,
        scratch_shapes=[
            pltpu.VMEM((FEATURES, (wide + 1) * leaf), BF16),
            pltpu.VMEM((FEATURES, cells + 2 * edge), BF16),
            pltpu.VMEM((rhs, (wide + 1) * leaf), F32),
            pltpu.SMEM((tasks,), jnp.int32),
            pltpu.SMEM((tasks,), jnp.int32),
        ],
        compiler_params=params,
        cost_estimate=pl.CostEstimate(
            flops=2 * 256 * 256 * 256 * 64 * 20, bytes_accessed=2 * 2**20, transcendentals=2**25
        ),
        name="near",
    )(
        counts,
        lists,
        list_left,
        list_right,
        points,
        points_left,
        points_right,
        vectors,
        vec_left,
        vec_right,
    )

    return pl.pallas_call(
        down_kernel,
        out_shape=jax.ShapeDtypeStruct((rhs, cells), F32),
        in_specs=[smem] + [vmem] * 9,
        out_specs=vmem,
        scratch_shapes=[
            pltpu.VMEM((3 * rows, rhs, 2 * rank), F32),
            pltpu.VMEM((2 * devices, rhs, 2 * rank), F32),
            pltpu.VMEM((leaf_dev // 2, rhs, 2 * rank), F32),
            pltpu.VMEM((leaf_dev // 2, rhs, 2 * rank), F32),
            pltpu.VMEM((2, rhs, edge), F32),
            pltpu.SemaphoreType.DMA((2,)),
            pltpu.SemaphoreType.DMA((2,)),
        ],
        compiler_params=pltpu.CompilerParams(
            vmem_limit_bytes=VMEM_BYTES, collective_id=1, has_side_effects=True
        ),
        cost_estimate=pl.CostEstimate(
            flops=2 * 256 * 256 * 256 * 64, bytes_accessed=4 * 2**20, transcendentals=2**21
        ),
        name="downward",
    )(
        far_list.T,
        near,
        leaf_basis,
        transfer,
        table,
        table_left,
        table_right,
        roots,
        transfer_top,
        skeleton_top,
    )


def solution(mesh):
    return jax.shard_map(
        body,
        mesh=mesh,
        in_specs=(
            P(None, "dev"),
            P(None, "dev"),
            P("dev", None, None),
            P("dev", None),
            P("dev", None),
            P("dev", None, None),
            P("dev", None),
            P(),
            P(),
        ),
        out_specs=P(None, "dev"),
        check_vma=False,
    )
```

```python
import math

import jax
import jax.numpy as jnp
from jax import lax
from jax.experimental import pallas as pl
from jax.experimental.pallas import tpu as pltpu
from jax.sharding import PartitionSpec as P

F32 = jnp.float32
BF16 = jnp.bfloat16
LOG2E = math.log2(math.e)
TINY = 1e-30
FEATURES = 48
GROUP = 8
STRIP = 64
MESH = pl.DeviceIdType.MESH
VMEM_BYTES = 56 * 1024 * 1024


def loop(count, unroll, step):
    unroll = min(unroll, count)

    def several(index, carry):
        for part in range(unroll):
            step(index * unroll + part)
        return carry

    lax.fori_loop(0, count // unroll, several, 0)


def level_row(leaf_count, level):
    return leaf_count - (leaf_count >> (level - 1))


def three_pieces(values):
    first = values.astype(BF16).astype(F32)
    rest = values - first
    second = rest.astype(BF16).astype(F32)
    return first, second, rest - second


def distance_factors(cells):
    row = lax.broadcasted_iota(jnp.int32, cells.shape, 0)
    scaled = jnp.where(row < 3, cells * LOG2E, 0.0)
    norms = jnp.sum(scaled * scaled, axis=0, keepdims=True)
    source = jnp.where(row == 3, norms, jnp.where(row == 4, 1.0, scaled))
    target = jnp.where(row == 3, 1.0, jnp.where(row == 4, norms, -2.0 * scaled))
    s1, s2, s3 = three_pieces(source)
    t1, t2, t3 = three_pieces(target)
    sources = jnp.concatenate([s1, s1, s2, s2, s1, s3], axis=0).astype(BF16)
    targets = jnp.concatenate([t1, t2, t1, t2, t3, t1], axis=0).astype(BF16)
    return sources, targets


def decay(squares):
    kept = jnp.maximum(squares, TINY)
    return jnp.exp2(-(kept * lax.rsqrt(kept)))


def product_rows(left, right):
    return lax.dot_general(left, right, (((0,), (0,)), ((), ())), preferred_element_type=F32)


def product(left, right):
    return lax.dot_general(left, right, (((1,), (0,)), ((), ())), preferred_element_type=F32)


def product_across(left, right):
    return lax.dot_general(left, right, (((1,), (1,)), ((), ())), preferred_element_type=F32)


def two_pieces(values):
    first = values.astype(BF16).astype(F32)
    return jnp.concatenate([first, values - first], axis=0).astype(BF16)


def fold(values):
    half = values.shape[0] // 2
    return values[:half] + values[half:]


def skeleton_cells(row):
    rank = row.shape[1] // 3
    parts = [row[:, c * rank : (c + 1) * rank] for c in range(3)]
    return jnp.concatenate(parts + [jnp.zeros((5, rank), F32)], axis=0)


def task_cells(offsets, rank):
    slots, leaf_dev = offsets.shape
    slot = lax.broadcasted_iota(jnp.int32, offsets.shape, 0)
    spot = lax.broadcasted_iota(jnp.int32, offsets.shape, 1)
    used = jnp.where((slot == 0) | (offsets != 0), 1.0, 0.0)
    lower = jnp.sum(jnp.where(spot < leaf_dev // 2, used, 0.0), keepdims=True)
    upper = jnp.sum(jnp.where(spot < leaf_dev // 2, 0.0, used), keepdims=True)
    row = lax.broadcasted_iota(jnp.int32, (8, rank), 0)
    column = lax.broadcasted_iota(jnp.int32, (8, rank), 1)
    counts = jnp.where(column == 0, lower, jnp.where(column == 1, upper, 0.0))
    return jnp.where(row == 5, counts, 0.0)


def up_kernel(
    list_ref,
    points_ref,
    vec_ref,
    basis_ref,
    transfer_ref,
    skeleton_ref,
    table_ref,
    table_left_ref,
    table_right_ref,
    roots_ref,
    points_left_ref,
    points_right_ref,
    vec_left_ref,
    vec_right_ref,
    list_left_ref,
    list_right_ref,
    pair_ref,
    send_sem,
    recv_sem,
    root_send_sem,
    root_recv_sem,
    own_sem,
):
    leaf_dev, rank, leaf = basis_ref.shape
    local = leaf_dev.bit_length() - 1
    rows = leaf_dev - 1
    devices = roots_ref.shape[0]
    me = lax.axis_index("dev")
    right = (me + 1) % devices
    left = (me + devices - 1) % devices
    has_right = me < devices - 1
    has_left = me > 0

    barrier = pltpu.get_barrier_semaphore()

    def greet(shift, carry):
        pl.semaphore_signal(
            barrier, inc=1, device_id=((me + shift) % devices,), device_id_type=MESH
        )
        return carry

    lax.fori_loop(1, devices, greet, 0)
    pl.semaphore_wait(barrier, devices - 1)

    def beside(source, arrival, device, index):
        return pltpu.make_async_remote_copy(
            src_ref=source,
            dst_ref=arrival,
            send_sem=send_sem.at[index],
            recv_sem=recv_sem.at[index],
            device_id=(device,),
            device_id_type=MESH,
        )

    leaf_right = [
        beside(points_ref, points_left_ref, right, 0),
        beside(vec_ref, vec_left_ref, right, 1),
        beside(list_ref, list_left_ref, right, 2),
    ]
    leaf_left = [
        beside(points_ref, points_right_ref, left, 3),
        beside(vec_ref, vec_right_ref, left, 4),
        beside(list_ref, list_right_ref, left, 5),
    ]
    table_right = beside(table_ref, table_left_ref, right, 6)
    table_left = beside(table_ref, table_right_ref, left, 7)

    @pl.when(has_right)
    def _():
        for copy in leaf_right:
            copy.start()

    @pl.when(has_left)
    def _():
        for copy in leaf_left:
            copy.start()

    def leaf_pair(pair):
        halves = []
        for part in range(2):
            spot = pair * 2 + part
            own = vec_ref[:, pl.ds(pl.multiple_of(spot * leaf, leaf), leaf)]
            halves.append(product_across(own, basis_ref[spot]))
        pair_ref[pair] = jnp.concatenate(halves, axis=1)

    loop(leaf_dev // 2, 8, leaf_pair)
    joined = [pair_ref[pair] for pair in range(leaf_dev // 2)]
    for level in range(1, local + 1):
        first = level_row(leaf_dev, level)
        coefs = []
        for spot in range(leaf_dev >> level):
            coef = fold(product_across(two_pieces(joined[spot]), transfer_ref[first + spot]))
            cells = skeleton_cells(skeleton_ref[pl.ds(first + spot, 1), :])
            if level == local:
                cells = cells + task_cells(list_ref[...], rank)
            table_ref[first + spot] = jnp.concatenate([coef, cells], axis=1)
            coefs.append(coef)
        joined = [
            jnp.concatenate(coefs[2 * spot : 2 * spot + 2], axis=1)
            for spot in range(len(coefs) // 2)
        ]

    root = table_ref.at[pl.ds(rows - 1, 1)]
    mine = roots_ref.at[pl.ds(me, 1)]

    def root_copy(shift):
        return pltpu.make_async_remote_copy(
            src_ref=root,
            dst_ref=mine,
            send_sem=root_send_sem.at[shift],
            recv_sem=root_recv_sem.at[shift],
            device_id=((me + shift) % devices,),
            device_id_type=MESH,
        )

    def send_root(shift, carry):
        root_copy(shift).start()
        return carry

    def wait_root(shift, carry):
        root_copy(shift).wait()
        return carry

    @pl.when(has_right)
    def _():
        table_right.start()

    @pl.when(has_left)
    def _():
        table_left.start()

    lax.fori_loop(1, devices, send_root, 0)
    own_copy = pltpu.make_async_copy(root, mine, own_sem)
    own_copy.start()

    @pl.when(has_right)
    def _():
        for copy in leaf_right + [table_right]:
            copy.wait_send()
        for copy in leaf_left + [table_left]:
            copy.wait_recv()

    @pl.when(has_left)
    def _():
        for copy in leaf_left + [table_left]:
            copy.wait_send()
        for copy in leaf_right + [table_right]:
            copy.wait_recv()

    lax.fori_loop(1, devices, wait_root, 0)
    own_copy.wait()


def balance(counts_ref, me):
    devices = counts_ref.shape[0]

    def total_and_most(spot, carry):
        total, most = carry
        own = counts_ref[spot, 0] + counts_ref[spot, 1]
        return total + own, jnp.maximum(most, own)

    total, most = lax.fori_loop(0, devices, total_and_most, (0, 0))

    def hand(spot, flow, limit):
        own = counts_ref[spot, 0] + counts_ref[spot, 1]
        after = jnp.minimum(spot + 1, devices - 1)
        lower = jnp.where(spot + 1 < devices, counts_ref[after, 0], 0)
        upper = jnp.where(spot + 1 < devices, counts_ref[spot, 1], 0)
        flow = jnp.maximum(own + flow - limit, -lower)
        return flow, jnp.where(flow <= upper, 1, 0)

    def halve(step, carry):
        low, high = carry
        limit = (low + high) >> 1

        def walk(spot, state):
            flow, fits = state
            flow, here = hand(spot, flow, limit)
            return flow, fits & here

        _, fits = lax.fori_loop(0, devices, walk, (0, 1))
        return jnp.where(fits == 1, low, limit + 1), jnp.where(fits == 1, limit, high)

    _, limit = lax.fori_loop(0, 6, halve, (total >> (devices.bit_length() - 1), most))
    before = lax.fori_loop(0, me, lambda spot, flow: hand(spot, flow, limit)[0], 0)
    return before, hand(me, before, limit)[0]


def near_kernel(
    counts_ref,
    list_ref,
    list_left_ref,
    list_right_ref,
    points_ref,
    points_left_ref,
    points_right_ref,
    vec_ref,
    vec_left_ref,
    vec_right_ref,
    out_ref,
    source_ref,
    target_ref,
    wide_vec_ref,
    task_target_ref,
    task_source_ref,
):
    slots, leaf_dev = list_ref.shape
    leaf = points_ref.shape[1] // leaf_dev
    half = leaf_dev // 2
    cells = leaf_dev * leaf
    edge = half * leaf
    wide = 3 * leaf_dev
    chunk = 4 * leaf
    me = lax.axis_index("dev")

    def fill(points, vecs, base, first, length, aimed):
        def step(index):
            start = pl.multiple_of(first + index * chunk, chunk)
            spot = pl.multiple_of(base + start, chunk)
            part = points[:, pl.ds(start, chunk)]
            part = jnp.concatenate([part, jnp.zeros((5, chunk), F32)], axis=0)
            sources, targets = distance_factors(part)
            source_ref[:, pl.ds(spot, chunk)] = sources
            if aimed:
                aim = pl.ds(pl.multiple_of(spot - edge, chunk), chunk)
                target_ref[:, aim] = targets
                out_ref[:, aim] = jnp.zeros((out_ref.shape[0], chunk), F32)
            wide_vec_ref[:, pl.ds(spot, chunk)] = vecs[:, pl.ds(start, chunk)].astype(F32)

        loop(length // chunk, 2, step)

    fill(points_left_ref, vec_left_ref, 0, 0, edge, False)
    fill(points_left_ref, vec_left_ref, 0, edge, edge, True)
    fill(points_ref, vec_ref, cells, 0, cells, True)
    fill(points_right_ref, vec_right_ref, 2 * cells, 0, edge, True)
    fill(points_right_ref, vec_right_ref, 2 * cells, edge, edge, False)
    empty = pl.ds(wide * leaf, leaf)
    source_ref[:, empty] = jnp.zeros((FEATURES, leaf), BF16)
    wide_vec_ref[:, empty] = jnp.zeros((wide_vec_ref.shape[0], leaf), F32)

    before, after = balance(counts_ref, me)

    def enlist(lists, base, first, last, low, high, count):
        def step(spot, carry):
            order, count = carry
            for slot in range(slots):
                offset = lists[slot, spot]
                task_target_ref[count] = base + spot - half
                task_source_ref[count] = base + spot + offset
                used = 1 if slot == 0 else jnp.where(offset != 0, 1, 0)
                kept = jnp.where((order >= low) & (order < high), used, 0)
                order = order + used
                count = count + kept
            return order, count

        return lax.fori_loop(first, last, step, (0, count))[1]

    before_upper = counts_ref[jnp.maximum(me - 1, 0), 1]
    own_tasks = counts_ref[me, 0] + counts_ref[me, 1]
    count = enlist(
        list_ref,
        leaf_dev,
        0,
        leaf_dev,
        jnp.maximum(-before, 0),
        own_tasks - jnp.maximum(after, 0),
        0,
    )
    count = enlist(
        list_left_ref,
        0,
        jnp.where(before > 0, half, leaf_dev),
        leaf_dev,
        before_upper - before,
        before_upper,
        count,
    )
    count = enlist(
        list_right_ref, 2 * leaf_dev, 0, jnp.where(after < 0, half, 0), 0, -after, count
    )
    for extra in range(GROUP):
        task_target_ref[count + extra] = 0
        task_source_ref[count + extra] = wide

    def several(index, carry):
        targets, vecs, factors = [], [], []
        for part in range(GROUP):
            target = pl.multiple_of(task_target_ref[index * GROUP + part] * leaf, leaf)
            source = pl.multiple_of(task_source_ref[index * GROUP + part] * leaf, leaf)
            targets.append(target)
            vecs.append(wide_vec_ref[:, pl.ds(source, leaf)].astype(BF16))
            factors.append((source_ref[:, pl.ds(source, leaf)], target_ref[:, pl.ds(target, leaf)]))
        strips = [(part, start) for part in range(GROUP) for start in range(0, leaf, STRIP)]
        tiles = [[] for _ in range(GROUP)]
        results = []
        ahead, standing = None, None
        for strip in strips + [None]:
            waiting, ahead = ahead, None
            if strip is not None:
                part, start = strip
                if start == 0:
                    standing = factors[part][0].T
                ahead = part, product(standing[start : start + STRIP], factors[part][1])
            if waiting is not None:
                part, squares = waiting
                tiles[part].append(decay(squares).astype(BF16))
                if len(tiles[part]) == leaf // STRIP:
                    results.append(product(vecs[part], jnp.concatenate(tiles[part], axis=0)))
        for target, result in zip(targets, results):
            out_ref[:, pl.ds(target, leaf)] += result
        return carry

    lax.fori_loop(0, (count + GROUP - 1) // GROUP, several, 0)


def couple(cells, rows, weights):
    rank = cells.shape[1]
    coefs = jnp.concatenate(
        [row[:, :rank] * weight for row, weight in zip(rows, weights)], axis=1
    )
    partner_cells = jnp.concatenate([row[:, rank:] for row in rows], axis=1)
    sources, _ = distance_factors(partner_cells)
    _, targets = distance_factors(cells)
    tile = decay(product_rows(sources, targets))
    main = tile.astype(BF16)
    rest = (tile - main.astype(F32)).astype(BF16)
    pieces = two_pieces(coefs)
    return fold(product(pieces, main) + product(pieces, rest))


def down_kernel(
    far_ref,
    near_ref,
    basis_ref,
    transfer_ref,
    own_ref,
    left_ref,
    right_ref,
    roots_ref,
    transfer_top_ref,
    skeleton_top_ref,
    out_ref,
    wide_ref,
    top_ref,
    coupled_ref,
    field_ref,
    help_ref,
    send_sem,
    recv_sem,
):
    leaf_dev, rank, leaf = basis_ref.shape
    devices = roots_ref.shape[0]
    local = leaf_dev.bit_length() - 1
    top = devices.bit_length() - 1
    rows = leaf_dev - 1
    me = lax.axis_index("dev")
    half = leaf_dev // 2
    edge = half * leaf
    has_right = me < devices - 1
    has_left = me > 0
    right = (me + 1) % devices
    left = (me + devices - 1) % devices

    barrier = pltpu.get_barrier_semaphore()

    @pl.when(has_right)
    def _():
        pl.semaphore_signal(barrier, inc=1, device_id=(right,), device_id_type=MESH)

    @pl.when(has_left)
    def _():
        pl.semaphore_signal(barrier, inc=1, device_id=(left,), device_id_type=MESH)

    pl.semaphore_wait(barrier, jnp.where(has_right, 1, 0) + jnp.where(has_left, 1, 0))

    def handed_back(start, index, device):
        return pltpu.make_async_remote_copy(
            src_ref=near_ref.at[:, pl.ds(start, edge)],
            dst_ref=help_ref.at[index],
            send_sem=send_sem.at[index],
            recv_sem=recv_sem.at[index],
            device_id=(device,),
            device_id_type=MESH,
        )

    to_right = handed_back(edge + leaf_dev * leaf, 0, right)
    to_left = handed_back(0, 1, left)

    @pl.when(has_right)
    def _():
        to_right.start()

    @pl.when(has_left)
    def _():
        to_left.start()

    for part, ref in enumerate((left_ref, own_ref, right_ref)):
        wide_ref[part * rows : (part + 1) * rows] = ref[...]
    top_ref[0:devices] = roots_ref[...]

    def top_row(step, spot):
        if step == 0:
            return spot
        return devices + devices - (devices >> (step - 1)) + spot

    for step in range(1, top):
        first = devices - (devices >> (step - 1))

        def lift(spot, step=step, first=first):
            joined = jnp.concatenate(
                [top_ref[top_row(step - 1, 2 * spot + part)][:, :rank] for part in range(2)],
                axis=1,
            )
            coef = fold(product_across(two_pieces(joined), transfer_top_ref[first + spot]))
            cells = skeleton_cells(skeleton_top_ref[pl.ds(first + spot, 1), :])
            top_ref[top_row(step, spot)] = jnp.concatenate([coef, cells], axis=1)

        loop(devices >> step, 16, lift)

    for level in range(1, local):
        first = level_row(leaf_dev, level)
        count = leaf_dev >> level

        def couple_pair(pair, first=first, count=count):
            halves = []
            for part in range(2):
                spot = pair * 2 + part
                partners, weights = [], []
                for slot in range(far_ref.shape[0]):
                    offset = far_ref[slot, first + spot]
                    partner = spot + offset
                    side = jnp.where(partner < 0, 0, jnp.where(partner < count, 1, 2))
                    partners.append(wide_ref[side * rows + first + partner - (side - 1) * count])
                    weights.append(jnp.where(offset != 0, 1.0, 0.0))
                mine = wide_ref[rows + first + spot]
                halves.append(couple(mine[:, rank:], partners, weights))
            coupled_ref[first // 2 + pair] = jnp.concatenate(halves, axis=1)

        loop(count // 2, 4, couple_pair)

    field = None
    for step in range(top - 1, -1, -1):
        spot = me >> step
        mine = top_ref[top_row(step, spot)]
        sibling = top_ref[top_row(step, spot ^ 1)]
        coupled = couple(mine[:, rank:], [sibling], [1.0])
        if field is None:
            field = coupled
        else:
            parent = devices - (devices >> step) + (spot >> 1)
            both = fold(product(two_pieces(field), transfer_top_ref[parent]))
            field = jnp.where((spot & 1) == 1, both[:, rank:], both[:, :rank]) + coupled

    fields = [field]
    for level in range(local - 1, -1, -1):
        first = level_row(leaf_dev, level + 1)
        below = []
        for spot, parent in enumerate(fields):
            both = fold(product(two_pieces(parent), transfer_ref[first + spot]))
            if level >= 1:
                both = both + coupled_ref[level_row(leaf_dev, level) // 2 + spot]
                below += [both[:, :rank], both[:, rank:]]
            else:
                field_ref[spot] = both
        fields = below

    @pl.when(has_right)
    def _():
        to_right.wait_send()
        to_left.wait_recv()

    @pl.when(has_left)
    def _():
        to_left.wait_send()
        to_right.wait_recv()

    @pl.when(jnp.logical_not(has_left))
    def _():
        help_ref[0] = jnp.zeros((help_ref.shape[1], edge), F32)

    @pl.when(jnp.logical_not(has_right))
    def _():
        help_ref[1] = jnp.zeros((help_ref.shape[1], edge), F32)

    for side in range(2):

        def expand(pair, side=side):
            both = field_ref[side * (half // 2) + pair]
            for part in range(2):
                spot = pair * 2 + part
                pieces = two_pieces(both[:, part * rank : (part + 1) * rank])
                inner = pl.multiple_of(spot * leaf, leaf)
                here = pl.multiple_of(side * edge + spot * leaf, leaf)
                there = pl.multiple_of(edge + side * edge + spot * leaf, leaf)
                near = near_ref[:, pl.ds(there, leaf)] + help_ref[side, :, pl.ds(inner, leaf)]
                far = fold(product(pieces, basis_ref[side * half + spot]))
                out_ref[:, pl.ds(here, leaf)] = near + far

        loop(half // 2, 4, expand)


def body(
    vectors, points, leaf_basis, near_list, far_list, transfer, skeleton, transfer_top, skeleton_top
):
    rhs, cells = vectors.shape
    leaf_dev, rank, leaf = leaf_basis.shape
    slots = near_list.shape[1]
    devices = lax.axis_size("dev")
    wide = 3 * leaf_dev
    edge = cells // 2
    rows = leaf_dev - 1
    vmem = pl.BlockSpec(memory_space=pltpu.VMEM)
    smem = pl.BlockSpec(memory_space=pltpu.SMEM)
    hbm = pl.BlockSpec(memory_space=pl.ANY)
    params = pltpu.CompilerParams(vmem_limit_bytes=VMEM_BYTES)

    table_shape = jax.ShapeDtypeStruct((rows, rhs, 2 * rank), F32)
    points_shape = jax.ShapeDtypeStruct(points.shape, points.dtype)
    lists = near_list.T
    list_shape = jax.ShapeDtypeStruct(lists.shape, lists.dtype)
    vec_shape = jax.ShapeDtypeStruct(vectors.shape, vectors.dtype)
    (
        table,
        table_left,
        table_right,
        roots,
        points_left,
        points_right,
        vec_left,
        vec_right,
        list_left,
        list_right,
    ) = pl.pallas_call(
        up_kernel,
        out_shape=(
            table_shape,
            table_shape,
            table_shape,
            jax.ShapeDtypeStruct((devices, rhs, 2 * rank), F32),
            points_shape,
            points_shape,
            vec_shape,
            vec_shape,
            list_shape,
            list_shape,
        ),
        in_specs=[vmem] * 6,
        out_specs=(vmem,) + (hbm,) * 9,
        scratch_shapes=[
            pltpu.VMEM((leaf_dev // 2, rhs, 2 * rank), F32),
            pltpu.SemaphoreType.DMA((8,)),
            pltpu.SemaphoreType.DMA((8,)),
            pltpu.SemaphoreType.DMA((devices,)),
            pltpu.SemaphoreType.DMA((devices,)),
            pltpu.SemaphoreType.DMA,
        ],
        compiler_params=pltpu.CompilerParams(
            vmem_limit_bytes=VMEM_BYTES, collective_id=0, has_side_effects=True
        ),
        cost_estimate=pl.CostEstimate(
            flops=2 * 256 * 256 * 256 * 64, bytes_accessed=4 * 2**20, transcendentals=0
        ),
        name="upward",
    )(lists, points, vectors, leaf_basis, transfer, skeleton)
    counts = roots[:, 5, rank : rank + 2].astype(jnp.int32)

    tasks = 2 * leaf_dev * slots + 2 * GROUP
    near = pl.pallas_call(
        near_kernel,
        out_shape=jax.ShapeDtypeStruct((rhs, cells + 2 * edge), F32),
        in_specs=[smem] * 4 + [vmem] * 6,
        out_specs=vmem,
        scratch_shapes=[
            pltpu.VMEM((FEATURES, (wide + 1) * leaf), BF16),
            pltpu.VMEM((FEATURES, cells + 2 * edge), BF16),
            pltpu.VMEM((rhs, (wide + 1) * leaf), F32),
            pltpu.SMEM((tasks,), jnp.int32),
            pltpu.SMEM((tasks,), jnp.int32),
        ],
        compiler_params=params,
        cost_estimate=pl.CostEstimate(
            flops=2 * 256 * 256 * 256 * 64 * 20, bytes_accessed=2 * 2**20, transcendentals=2**25
        ),
        name="near",
    )(
        counts,
        lists,
        list_left,
        list_right,
        points,
        points_left,
        points_right,
        vectors,
        vec_left,
        vec_right,
    )

    return pl.pallas_call(
        down_kernel,
        out_shape=jax.ShapeDtypeStruct((rhs, cells), F32),
        in_specs=[smem] + [vmem] * 9,
        out_specs=vmem,
        scratch_shapes=[
            pltpu.VMEM((3 * rows, rhs, 2 * rank), F32),
            pltpu.VMEM((2 * devices, rhs, 2 * rank), F32),
            pltpu.VMEM((leaf_dev // 2, rhs, 2 * rank), F32),
            pltpu.VMEM((leaf_dev // 2, rhs, 2 * rank), F32),
            pltpu.VMEM((2, rhs, edge), F32),
            pltpu.SemaphoreType.DMA((2,)),
            pltpu.SemaphoreType.DMA((2,)),
        ],
        compiler_params=pltpu.CompilerParams(
            vmem_limit_bytes=VMEM_BYTES, collective_id=1, has_side_effects=True
        ),
        cost_estimate=pl.CostEstimate(
            flops=2 * 256 * 256 * 256 * 64, bytes_accessed=4 * 2**20, transcendentals=2**21
        ),
        name="downward",
    )(
        far_list.T,
        near,
        leaf_basis,
        transfer,
        table,
        table_left,
        table_right,
        roots,
        transfer_top,
        skeleton_top,
    )


def solution(mesh):
    return jax.shard_map(
        body,
        mesh=mesh,
        in_specs=(
            P(None, "dev"),
            P(None, "dev"),
            P("dev", None, None),
            P("dev", None),
            P("dev", None),
            P("dev", None, None),
            P("dev", None),
            P(),
            P(),
        ),
        out_specs=P(None, "dev"),
        check_vma=False,
    )
```

```python
import math

import jax
import jax.numpy as jnp
from jax import lax
from jax.experimental import pallas as pl
from jax.experimental.pallas import tpu as pltpu
from jax.sharding import PartitionSpec as P

F32 = jnp.float32
BF16 = jnp.bfloat16
LOG2E = math.log2(math.e)
TINY = 1e-30
FEATURES = 48
GROUP = 8
STRIP = 64
MESH = pl.DeviceIdType.MESH
VMEM_BYTES = 56 * 1024 * 1024


def loop(count, unroll, step):
    unroll = min(unroll, count)

    def several(index, carry):
        for part in range(unroll):
            step(index * unroll + part)
        return carry

    lax.fori_loop(0, count // unroll, several, 0)


def level_row(leaf_count, level):
    return leaf_count - (leaf_count >> (level - 1))


def three_pieces(values):
    first = values.astype(BF16).astype(F32)
    rest = values - first
    second = rest.astype(BF16).astype(F32)
    return first, second, rest - second


def distance_factors(cells):
    row = lax.broadcasted_iota(jnp.int32, cells.shape, 0)
    scaled = jnp.where(row < 3, cells * LOG2E, 0.0)
    norms = jnp.sum(scaled * scaled, axis=0, keepdims=True)
    source = jnp.where(row == 3, norms, jnp.where(row == 4, 1.0, scaled))
    target = jnp.where(row == 3, 1.0, jnp.where(row == 4, norms, -2.0 * scaled))
    s1, s2, s3 = three_pieces(source)
    t1, t2, t3 = three_pieces(target)
    sources = jnp.concatenate([s1, s1, s2, s2, s1, s3], axis=0).astype(BF16)
    targets = jnp.concatenate([t1, t2, t1, t2, t3, t1], axis=0).astype(BF16)
    return sources, targets


def decay(squares):
    kept = jnp.maximum(squares, TINY)
    return jnp.exp2(-(kept * lax.rsqrt(kept)))


def product_rows(left, right):
    return lax.dot_general(left, right, (((0,), (0,)), ((), ())), preferred_element_type=F32)


def product(left, right):
    return lax.dot_general(left, right, (((1,), (0,)), ((), ())), preferred_element_type=F32)


def product_across(left, right):
    return lax.dot_general(left, right, (((1,), (1,)), ((), ())), preferred_element_type=F32)


def two_pieces(values):
    first = values.astype(BF16).astype(F32)
    return jnp.concatenate([first, values - first], axis=0).astype(BF16)


def fold(values):
    half = values.shape[0] // 2
    return values[:half] + values[half:]


def skeleton_cells(row):
    rank = row.shape[1] // 3
    parts = [row[:, c * rank : (c + 1) * rank] for c in range(3)]
    return jnp.concatenate(parts + [jnp.zeros((5, rank), F32)], axis=0)


def task_cells(offsets, rank):
    slots, leaf_dev = offsets.shape
    slot = lax.broadcasted_iota(jnp.int32, offsets.shape, 0)
    spot = lax.broadcasted_iota(jnp.int32, offsets.shape, 1)
    used = jnp.where((slot == 0) | (offsets != 0), 1.0, 0.0)
    lower = jnp.sum(jnp.where(spot < leaf_dev // 2, used, 0.0), keepdims=True)
    upper = jnp.sum(jnp.where(spot < leaf_dev // 2, 0.0, used), keepdims=True)
    row = lax.broadcasted_iota(jnp.int32, (8, rank), 0)
    column = lax.broadcasted_iota(jnp.int32, (8, rank), 1)
    counts = jnp.where(column == 0, lower, jnp.where(column == 1, upper, 0.0))
    return jnp.where(row == 5, counts, 0.0)


def up_kernel(
    list_ref,
    points_ref,
    vec_ref,
    basis_ref,
    transfer_ref,
    skeleton_ref,
    table_ref,
    roots_ref,
    points_left_ref,
    points_right_ref,
    vec_left_ref,
    vec_right_ref,
    list_left_ref,
    list_right_ref,
    pair_ref,
    send_sem,
    recv_sem,
    root_send_sem,
    root_recv_sem,
    own_sem,
):
    leaf_dev, rank, leaf = basis_ref.shape
    local = leaf_dev.bit_length() - 1
    rows = leaf_dev - 1
    devices = roots_ref.shape[0]
    me = lax.axis_index("dev")
    right = (me + 1) % devices
    left = (me + devices - 1) % devices
    has_right = me < devices - 1
    has_left = me > 0

    barrier = pltpu.get_barrier_semaphore()

    def greet(shift, carry):
        pl.semaphore_signal(
            barrier, inc=1, device_id=((me + shift) % devices,), device_id_type=MESH
        )
        return carry

    lax.fori_loop(1, devices, greet, 0)
    pl.semaphore_wait(barrier, devices - 1)

    def beside(source, arrival, device, index):
        return pltpu.make_async_remote_copy(
            src_ref=source,
            dst_ref=arrival,
            send_sem=send_sem.at[index],
            recv_sem=recv_sem.at[index],
            device_id=(device,),
            device_id_type=MESH,
        )

    leaf_right = [
        beside(points_ref, points_left_ref, right, 0),
        beside(vec_ref, vec_left_ref, right, 1),
        beside(list_ref, list_left_ref, right, 2),
    ]
    leaf_left = [
        beside(points_ref, points_right_ref, left, 3),
        beside(vec_ref, vec_right_ref, left, 4),
        beside(list_ref, list_right_ref, left, 5),
    ]

    @pl.when(has_right)
    def _():
        for copy in leaf_right:
            copy.start()

    @pl.when(has_left)
    def _():
        for copy in leaf_left:
            copy.start()

    def leaf_pair(pair):
        halves = []
        for part in range(2):
            spot = pair * 2 + part
            own = vec_ref[:, pl.ds(pl.multiple_of(spot * leaf, leaf), leaf)]
            halves.append(product_across(own, basis_ref[spot]))
        pair_ref[pair] = jnp.concatenate(halves, axis=1)

    loop(leaf_dev // 2, 8, leaf_pair)
    joined = [pair_ref[pair] for pair in range(leaf_dev // 2)]
    for level in range(1, local + 1):
        first = level_row(leaf_dev, level)
        coefs = []
        for spot in range(leaf_dev >> level):
            coef = fold(product_across(two_pieces(joined[spot]), transfer_ref[first + spot]))
            cells = skeleton_cells(skeleton_ref[pl.ds(first + spot, 1), :])
            if level == local:
                cells = cells + task_cells(list_ref[...], rank)
            table_ref[first + spot] = jnp.concatenate([coef, cells], axis=1)
            coefs.append(coef)
        joined = [
            jnp.concatenate(coefs[2 * spot : 2 * spot + 2], axis=1)
            for spot in range(len(coefs) // 2)
        ]

    root = table_ref.at[pl.ds(rows - 1, 1)]
    mine = roots_ref.at[pl.ds(me, 1)]

    def root_copy(shift):
        return pltpu.make_async_remote_copy(
            src_ref=root,
            dst_ref=mine,
            send_sem=root_send_sem.at[shift],
            recv_sem=root_recv_sem.at[shift],
            device_id=((me + shift) % devices,),
            device_id_type=MESH,
        )

    def send_root(shift, carry):
        root_copy(shift).start()
        return carry

    def wait_root(shift, carry):
        root_copy(shift).wait()
        return carry

    lax.fori_loop(1, devices, send_root, 0)
    own_copy = pltpu.make_async_copy(root, mine, own_sem)
    own_copy.start()

    @pl.when(has_right)
    def _():
        for copy in leaf_right:
            copy.wait_send()
        for copy in leaf_left:
            copy.wait_recv()

    @pl.when(has_left)
    def _():
        for copy in leaf_left:
            copy.wait_send()
        for copy in leaf_right:
            copy.wait_recv()

    lax.fori_loop(1, devices, wait_root, 0)
    own_copy.wait()


def balance(counts_ref, me):
    devices = counts_ref.shape[0]

    def total_and_most(spot, carry):
        total, most = carry
        own = counts_ref[spot, 0] + counts_ref[spot, 1]
        return total + own, jnp.maximum(most, own)

    total, most = lax.fori_loop(0, devices, total_and_most, (0, 0))

    def hand(spot, flow, limit):
        own = counts_ref[spot, 0] + counts_ref[spot, 1]
        after = jnp.minimum(spot + 1, devices - 1)
        lower = jnp.where(spot + 1 < devices, counts_ref[after, 0], 0)
        upper = jnp.where(spot + 1 < devices, counts_ref[spot, 1], 0)
        flow = jnp.maximum(own + flow - limit, -lower)
        return flow, jnp.where(flow <= upper, 1, 0)

    def halve(step, carry):
        low, high = carry
        limit = (low + high) >> 1

        def walk(spot, state):
            flow, fits = state
            flow, here = hand(spot, flow, limit)
            return flow, fits & here

        _, fits = lax.fori_loop(0, devices, walk, (0, 1))
        return jnp.where(fits == 1, low, limit + 1), jnp.where(fits == 1, limit, high)

    _, limit = lax.fori_loop(0, 6, halve, (total >> (devices.bit_length() - 1), most))
    before = lax.fori_loop(0, me, lambda spot, flow: hand(spot, flow, limit)[0], 0)
    return before, hand(me, before, limit)[0]


def near_kernel(
    counts_ref,
    list_ref,
    list_left_ref,
    list_right_ref,
    points_ref,
    points_left_ref,
    points_right_ref,
    vec_ref,
    vec_left_ref,
    vec_right_ref,
    out_ref,
    source_ref,
    target_ref,
    wide_vec_ref,
    task_target_ref,
    task_source_ref,
):
    slots, leaf_dev = list_ref.shape
    leaf = points_ref.shape[1] // leaf_dev
    half = leaf_dev // 2
    cells = leaf_dev * leaf
    edge = half * leaf
    wide = 3 * leaf_dev
    chunk = 4 * leaf
    me = lax.axis_index("dev")

    def fill(points, vecs, base, first, length, aimed):
        def step(index):
            start = pl.multiple_of(first + index * chunk, chunk)
            spot = pl.multiple_of(base + start, chunk)
            part = points[:, pl.ds(start, chunk)]
            part = jnp.concatenate([part, jnp.zeros((5, chunk), F32)], axis=0)
            sources, targets = distance_factors(part)
            source_ref[:, pl.ds(spot, chunk)] = sources
            if aimed:
                aim = pl.ds(pl.multiple_of(spot - edge, chunk), chunk)
                target_ref[:, aim] = targets
                out_ref[:, aim] = jnp.zeros((out_ref.shape[0], chunk), F32)
            wide_vec_ref[:, pl.ds(spot, chunk)] = vecs[:, pl.ds(start, chunk)].astype(F32)

        loop(length // chunk, 2, step)

    fill(points_left_ref, vec_left_ref, 0, 0, edge, False)
    fill(points_left_ref, vec_left_ref, 0, edge, edge, True)
    fill(points_ref, vec_ref, cells, 0, cells, True)
    fill(points_right_ref, vec_right_ref, 2 * cells, 0, edge, True)
    fill(points_right_ref, vec_right_ref, 2 * cells, edge, edge, False)
    empty = pl.ds(wide * leaf, leaf)
    source_ref[:, empty] = jnp.zeros((FEATURES, leaf), BF16)
    wide_vec_ref[:, empty] = jnp.zeros((wide_vec_ref.shape[0], leaf), F32)

    before, after = balance(counts_ref, me)

    def enlist(lists, base, first, last, low, high, count):
        def step(spot, carry):
            order, count = carry
            for slot in range(slots):
                offset = lists[slot, spot]
                task_target_ref[count] = base + spot - half
                task_source_ref[count] = base + spot + offset
                used = 1 if slot == 0 else jnp.where(offset != 0, 1, 0)
                kept = jnp.where((order >= low) & (order < high), used, 0)
                order = order + used
                count = count + kept
            return order, count

        return lax.fori_loop(first, last, step, (0, count))[1]

    before_upper = counts_ref[jnp.maximum(me - 1, 0), 1]
    own_tasks = counts_ref[me, 0] + counts_ref[me, 1]
    count = enlist(
        list_ref,
        leaf_dev,
        0,
        leaf_dev,
        jnp.maximum(-before, 0),
        own_tasks - jnp.maximum(after, 0),
        0,
    )
    count = enlist(
        list_left_ref,
        0,
        jnp.where(before > 0, half, leaf_dev),
        leaf_dev,
        before_upper - before,
        before_upper,
        count,
    )
    count = enlist(
        list_right_ref, 2 * leaf_dev, 0, jnp.where(after < 0, half, 0), 0, -after, count
    )
    for extra in range(GROUP):
        task_target_ref[count + extra] = 0
        task_source_ref[count + extra] = wide

    def several(index, carry):
        targets, vecs, factors = [], [], []
        for part in range(GROUP):
            target = pl.multiple_of(task_target_ref[index * GROUP + part] * leaf, leaf)
            source = pl.multiple_of(task_source_ref[index * GROUP + part] * leaf, leaf)
            targets.append(target)
            vecs.append(wide_vec_ref[:, pl.ds(source, leaf)].astype(BF16))
            factors.append((source_ref[:, pl.ds(source, leaf)], target_ref[:, pl.ds(target, leaf)]))
        strips = [(part, start) for part in range(GROUP) for start in range(0, leaf, STRIP)]
        tiles = [[] for _ in range(GROUP)]
        results = []
        ahead, standing = None, None
        for strip in strips + [None]:
            waiting, ahead = ahead, None
            if strip is not None:
                part, start = strip
                if start == 0:
                    standing = factors[part][0].T
                ahead = part, product(standing[start : start + STRIP], factors[part][1])
            if waiting is not None:
                part, squares = waiting
                tiles[part].append(decay(squares).astype(BF16))
                if len(tiles[part]) == leaf // STRIP:
                    results.append(product(vecs[part], jnp.concatenate(tiles[part], axis=0)))
        for target, result in zip(targets, results):
            out_ref[:, pl.ds(target, leaf)] += result
        return carry

    lax.fori_loop(0, (count + GROUP - 1) // GROUP, several, 0)


def couple(cells, rows, weights):
    rank = cells.shape[1]
    coefs = jnp.concatenate(
        [row[:, :rank] * weight for row, weight in zip(rows, weights)], axis=1
    )
    partner_cells = jnp.concatenate([row[:, rank:] for row in rows], axis=1)
    sources, _ = distance_factors(partner_cells)
    _, targets = distance_factors(cells)
    tile = decay(product_rows(sources, targets))
    main = tile.astype(BF16)
    rest = (tile - main.astype(F32)).astype(BF16)
    pieces = two_pieces(coefs)
    return fold(product(pieces, main) + product(pieces, rest))


def down_kernel(
    far_ref,
    near_ref,
    basis_ref,
    transfer_ref,
    own_ref,
    roots_ref,
    transfer_top_ref,
    skeleton_top_ref,
    out_ref,
    wide_ref,
    top_ref,
    coupled_ref,
    field_ref,
    help_ref,
    send_sem,
    recv_sem,
):
    leaf_dev, rank, leaf = basis_ref.shape
    devices = roots_ref.shape[0]
    local = leaf_dev.bit_length() - 1
    top = devices.bit_length() - 1
    rows = leaf_dev - 1
    me = lax.axis_index("dev")
    half = leaf_dev // 2
    edge = half * leaf
    has_right = me < devices - 1
    has_left = me > 0
    right = (me + 1) % devices
    left = (me + devices - 1) % devices

    barrier = pltpu.get_barrier_semaphore()

    @pl.when(has_right)
    def _():
        pl.semaphore_signal(barrier, inc=1, device_id=(right,), device_id_type=MESH)

    @pl.when(has_left)
    def _():
        pl.semaphore_signal(barrier, inc=1, device_id=(left,), device_id_type=MESH)

    pl.semaphore_wait(barrier, jnp.where(has_right, 1, 0) + jnp.where(has_left, 1, 0))

    def beside(source, arrival, index, device):
        return pltpu.make_async_remote_copy(
            src_ref=source,
            dst_ref=arrival,
            send_sem=send_sem.at[index],
            recv_sem=recv_sem.at[index],
            device_id=(device,),
            device_id_type=MESH,
        )

    upper = near_ref.at[:, pl.ds(edge + leaf_dev * leaf, edge)]
    lower = near_ref.at[:, pl.ds(0, edge)]
    to_right = beside(upper, help_ref.at[0], 0, right)
    to_left = beside(lower, help_ref.at[1], 1, left)
    table_right = beside(own_ref, wide_ref.at[pl.ds(0, rows)], 2, right)
    table_left = beside(own_ref, wide_ref.at[pl.ds(2 * rows, rows)], 3, left)

    @pl.when(has_right)
    def _():
        table_right.start()
        to_right.start()

    @pl.when(has_left)
    def _():
        table_left.start()
        to_left.start()

    wide_ref[rows : 2 * rows] = own_ref[...]
    top_ref[0:devices] = roots_ref[...]

    def top_row(step, spot):
        if step == 0:
            return spot
        return devices + devices - (devices >> (step - 1)) + spot

    for step in range(1, top):
        first = devices - (devices >> (step - 1))

        def lift(spot, step=step, first=first):
            joined = jnp.concatenate(
                [top_ref[top_row(step - 1, 2 * spot + part)][:, :rank] for part in range(2)],
                axis=1,
            )
            coef = fold(product_across(two_pieces(joined), transfer_top_ref[first + spot]))
            cells = skeleton_cells(skeleton_top_ref[pl.ds(first + spot, 1), :])
            top_ref[top_row(step, spot)] = jnp.concatenate([coef, cells], axis=1)

        loop(devices >> step, 16, lift)

    field = None
    for step in range(top - 1, -1, -1):
        spot = me >> step
        mine = top_ref[top_row(step, spot)]
        sibling = top_ref[top_row(step, spot ^ 1)]
        coupled = couple(mine[:, rank:], [sibling], [1.0])
        if field is None:
            field = coupled
        else:
            parent = devices - (devices >> step) + (spot >> 1)
            both = fold(product(two_pieces(field), transfer_top_ref[parent]))
            field = jnp.where((spot & 1) == 1, both[:, rank:], both[:, :rank]) + coupled

    @pl.when(has_right)
    def _():
        table_right.wait_send()
        table_left.wait_recv()

    @pl.when(has_left)
    def _():
        table_left.wait_send()
        table_right.wait_recv()

    @pl.when(jnp.logical_not(has_left))
    def _():
        wide_ref[0:rows] = jnp.zeros(own_ref.shape, F32)

    @pl.when(jnp.logical_not(has_right))
    def _():
        wide_ref[2 * rows : 3 * rows] = jnp.zeros(own_ref.shape, F32)

    for level in range(1, local):
        first = level_row(leaf_dev, level)
        count = leaf_dev >> level

        def couple_pair(pair, first=first, count=count):
            halves = []
            for part in range(2):
                spot = pair * 2 + part
                partners, weights = [], []
                for slot in range(far_ref.shape[0]):
                    offset = far_ref[slot, first + spot]
                    partner = spot + offset
                    side = jnp.where(partner < 0, 0, jnp.where(partner < count, 1, 2))
                    partners.append(wide_ref[side * rows + first + partner - (side - 1) * count])
                    weights.append(jnp.where(offset != 0, 1.0, 0.0))
                mine = wide_ref[rows + first + spot]
                halves.append(couple(mine[:, rank:], partners, weights))
            coupled_ref[first // 2 + pair] = jnp.concatenate(halves, axis=1)

        loop(count // 2, 4, couple_pair)

    fields = [field]
    for level in range(local - 1, -1, -1):
        first = level_row(leaf_dev, level + 1)
        below = []
        for spot, parent in enumerate(fields):
            both = fold(product(two_pieces(parent), transfer_ref[first + spot]))
            if level >= 1:
                both = both + coupled_ref[level_row(leaf_dev, level) // 2 + spot]
                below += [both[:, :rank], both[:, rank:]]
            else:
                field_ref[spot] = both
        fields = below

    @pl.when(has_right)
    def _():
        to_right.wait_send()
        to_left.wait_recv()

    @pl.when(has_left)
    def _():
        to_left.wait_send()
        to_right.wait_recv()

    @pl.when(jnp.logical_not(has_left))
    def _():
        help_ref[0] = jnp.zeros((help_ref.shape[1], edge), F32)

    @pl.when(jnp.logical_not(has_right))
    def _():
        help_ref[1] = jnp.zeros((help_ref.shape[1], edge), F32)

    for side in range(2):

        def expand(pair, side=side):
            both = field_ref[side * (half // 2) + pair]
            for part in range(2):
                spot = pair * 2 + part
                pieces = two_pieces(both[:, part * rank : (part + 1) * rank])
                inner = pl.multiple_of(spot * leaf, leaf)
                here = pl.multiple_of(side * edge + spot * leaf, leaf)
                there = pl.multiple_of(edge + side * edge + spot * leaf, leaf)
                near = near_ref[:, pl.ds(there, leaf)] + help_ref[side, :, pl.ds(inner, leaf)]
                far = fold(product(pieces, basis_ref[side * half + spot]))
                out_ref[:, pl.ds(here, leaf)] = near + far

        loop(half // 2, 4, expand)


def body(
    vectors, points, leaf_basis, near_list, far_list, transfer, skeleton, transfer_top, skeleton_top
):
    rhs, cells = vectors.shape
    leaf_dev, rank, leaf = leaf_basis.shape
    slots = near_list.shape[1]
    devices = lax.axis_size("dev")
    wide = 3 * leaf_dev
    edge = cells // 2
    rows = leaf_dev - 1
    vmem = pl.BlockSpec(memory_space=pltpu.VMEM)
    smem = pl.BlockSpec(memory_space=pltpu.SMEM)
    hbm = pl.BlockSpec(memory_space=pl.ANY)
    params = pltpu.CompilerParams(vmem_limit_bytes=VMEM_BYTES)

    table_shape = jax.ShapeDtypeStruct((rows, rhs, 2 * rank), F32)
    points_shape = jax.ShapeDtypeStruct(points.shape, points.dtype)
    lists = near_list.T
    list_shape = jax.ShapeDtypeStruct(lists.shape, lists.dtype)
    vec_shape = jax.ShapeDtypeStruct(vectors.shape, vectors.dtype)
    (
        table,
        roots,
        points_left,
        points_right,
        vec_left,
        vec_right,
        list_left,
        list_right,
    ) = pl.pallas_call(
        up_kernel,
        out_shape=(
            table_shape,
            jax.ShapeDtypeStruct((devices, rhs, 2 * rank), F32),
            points_shape,
            points_shape,
            vec_shape,
            vec_shape,
            list_shape,
            list_shape,
        ),
        in_specs=[vmem] * 6,
        out_specs=(vmem,) + (hbm,) * 7,
        scratch_shapes=[
            pltpu.VMEM((leaf_dev // 2, rhs, 2 * rank), F32),
            pltpu.SemaphoreType.DMA((6,)),
            pltpu.SemaphoreType.DMA((6,)),
            pltpu.SemaphoreType.DMA((devices,)),
            pltpu.SemaphoreType.DMA((devices,)),
            pltpu.SemaphoreType.DMA,
        ],
        compiler_params=pltpu.CompilerParams(
            vmem_limit_bytes=VMEM_BYTES, collective_id=0, has_side_effects=True
        ),
        cost_estimate=pl.CostEstimate(
            flops=2 * 256 * 256 * 256 * 64, bytes_accessed=4 * 2**20, transcendentals=0
        ),
        name="upward",
    )(lists, points, vectors, leaf_basis, transfer, skeleton)
    counts = roots[:, 5, rank : rank + 2].astype(jnp.int32)

    tasks = 2 * leaf_dev * slots + 2 * GROUP
    near = pl.pallas_call(
        near_kernel,
        out_shape=jax.ShapeDtypeStruct((rhs, cells + 2 * edge), F32),
        in_specs=[smem] * 4 + [vmem] * 6,
        out_specs=vmem,
        scratch_shapes=[
            pltpu.VMEM((FEATURES, (wide + 1) * leaf), BF16),
            pltpu.VMEM((FEATURES, cells + 2 * edge), BF16),
            pltpu.VMEM((rhs, (wide + 1) * leaf), F32),
            pltpu.SMEM((tasks,), jnp.int32),
            pltpu.SMEM((tasks,), jnp.int32),
        ],
        compiler_params=params,
        cost_estimate=pl.CostEstimate(
            flops=2 * 256 * 256 * 256 * 64 * 20, bytes_accessed=2 * 2**20, transcendentals=2**25
        ),
        name="near",
    )(
        counts,
        lists,
        list_left,
        list_right,
        points,
        points_left,
        points_right,
        vectors,
        vec_left,
        vec_right,
    )

    return pl.pallas_call(
        down_kernel,
        out_shape=jax.ShapeDtypeStruct((rhs, cells), F32),
        in_specs=[smem] + [vmem] * 7,
        out_specs=vmem,
        scratch_shapes=[
            pltpu.VMEM((3 * rows, rhs, 2 * rank), F32),
            pltpu.VMEM((2 * devices, rhs, 2 * rank), F32),
            pltpu.VMEM((leaf_dev // 2, rhs, 2 * rank), F32),
            pltpu.VMEM((leaf_dev // 2, rhs, 2 * rank), F32),
            pltpu.VMEM((2, rhs, edge), F32),
            pltpu.SemaphoreType.DMA((4,)),
            pltpu.SemaphoreType.DMA((4,)),
        ],
        compiler_params=pltpu.CompilerParams(
            vmem_limit_bytes=VMEM_BYTES, collective_id=1, has_side_effects=True
        ),
        cost_estimate=pl.CostEstimate(
            flops=2 * 256 * 256 * 256 * 64, bytes_accessed=4 * 2**20, transcendentals=2**21
        ),
        name="downward",
    )(
        far_list.T,
        near,
        leaf_basis,
        transfer,
        table,
        roots,
        transfer_top,
        skeleton_top,
    )


def solution(mesh):
    return jax.shard_map(
        body,
        mesh=mesh,
        in_specs=(
            P(None, "dev"),
            P(None, "dev"),
            P("dev", None, None),
            P("dev", None),
            P("dev", None),
            P("dev", None, None),
            P("dev", None),
            P(),
            P(),
        ),
        out_specs=P(None, "dev"),
        check_vma=False,
    )
```
